256 devices in a mesh: patch: 16 (over x, y), layer: 16 (over z, core).
Axes of the slice: x: 4, y: 4, z: 8, core: 2. Of those that a mesh axis runs over, the one named last changes fastest.
Arguments:
- polarization: float32 [3, 128, 1024, 128], P(None, 'patch', 'layer'), may hold values from -2.5 to 2.5
- quadratic: float32 [128, 1024, 128], P('patch', 'layer'), may hold values from -1.5 to -0.2
- neighbours: int32 [4, 128], P(None, 'patch'), may hold values from 0 to 127, as said below
- refinement: int32 [128], P('patch'), may hold values from 0 to 2
Outputs:
- final_polarization: float32 [3, 128, 1024, 128], P(None, 'patch', 'layer')
- depolarizing: float32 [128, 1024, 128], P('patch', 'layer')
The draws below stay inside these ranges and needn't reach their ends.
Inputs may be any that keep to these rules, and one draw needn't show every extreme that they name: The face graph is symmetric: neighbours[1, neighbours[0, s]] = s and neighbours[0, neighbours[1, s]] = s, and likewise for 2 and 3. At most 2 of the 32 entries of one device's patches name patches of any single other device, a bound reached in every draw.
All inputs are finite; a program needn't handle non-finite values.
Results may differ from the reference program's by a relative error of at most 0.000026.
Values sent between devices are 32-bit elements; how exact they have to be, the bound alone decides.
A program may use at most 128 MiB of HBM per device.

```python
import math
import jax
import jax.numpy as jnp

P_DEV = 8
NZ = 1024
PATCHES = 128
N_PATCH = 16


def draw_polarization(key, part):
    key = jax.random.fold_in(key, 9)
    array_shape = (3, PATCHES, NZ, 128)
    return jnp.clip(0.6 * jax.random.normal(key, array_shape, jnp.float32), -2.5, 2.5)


def face_links(order_key, last_offset):
    order_keys = jax.random.split(order_key, N_PATCH)
    slot_orders = jax.vmap(jax.random.permutation, in_axes=(0, None))(order_keys, P_DEV)
    device_ids = jnp.arange(N_PATCH, dtype=jnp.int32)[:, None]
    rank_ids = jnp.broadcast_to(jnp.arange(P_DEV, dtype=jnp.int32)[None, :], (N_PATCH, P_DEV))
    if 2 * P_DEV <= N_PATCH:
        offsets = jnp.where(rank_ids == P_DEV - 1, last_offset, rank_ids).astype(jnp.int32)
    else:
        offsets = rank_ids % N_PATCH
    source_slot = device_ids * P_DEV + slot_orders
    target_device = (device_ids + offsets) % N_PATCH
    target_slot = target_device * P_DEV + slot_orders[target_device, rank_ids]
    forward = jnp.zeros((PATCHES,), jnp.int32).at[source_slot.reshape(-1)].set(target_slot.reshape(-1).astype(jnp.int32))
    backward = jnp.zeros((PATCHES,), jnp.int32).at[target_slot.reshape(-1)].set(source_slot.reshape(-1).astype(jnp.int32))
    return (forward, backward)


def draw_neighbours(key, part):
    key = jax.random.fold_in(key, 5)
    key_rows, key_cols = jax.random.split(key)
    row_low, row_high = face_links(key_rows, N_PATCH // 2)
    col_low, col_high = face_links(key_cols, P_DEV - 1)
    return jnp.stack([row_low, row_high, col_low, col_high]).astype(jnp.int32)


def with_ends(result, key, smallest, top_value):
    place = [jax.random.randint(jax.random.fold_in(key, axis), (), 0, length) for axis, length in enumerate(result.shape)]
    longest = result.shape.index(max(result.shape))
    next_to = place[:longest] + [(place[longest] + 1) % result.shape[longest]] + place[longest + 1:]
    return result.at[tuple(place)].set(smallest).at[tuple(next_to)].set(top_value)


def block_scale(own_key, shape, cuts, least, top_value):
    def one(position, shards_of):
        steps = jax.random.uniform(jax.random.fold_in(jax.random.fold_in(own_key, 6), position), (shards_of,), jnp.float32, least / len(cuts), top_value / len(cuts))
        return jnp.repeat(jnp.exp(steps), shape[position] // shards_of).reshape((-1,) + (1,) * (len(shape) - position - 1))

    loudness = one(*cuts[0])
    for cut in cuts[1:]:
        loudness = loudness * one(*cut)
    return loudness


def setup_inputs(seed: int = 0) -> dict:
    seeds = jax.random.split(jax.random.key(seed), 5)
    return {
        "polarization": draw_polarization(jax.random.fold_in(seeds[4], 71), 0),
        "quadratic": jnp.clip(-1.5 + 1.3 * jax.random.uniform(seeds[1], (PATCHES, NZ, 128), jnp.float32) ** block_scale(seeds[1], (PATCHES, NZ, 128), ((0, 16), (1, 16)), -0.2, 0.2), -1.5, -0.2),
        "neighbours": draw_neighbours(jax.random.fold_in(seeds[4], 71), 0),
        "refinement": with_ends(jax.random.randint(seeds[3], (PATCHES,), 0, 3), jax.random.fold_in(seeds[3], 1), 0, 2).astype(jnp.int32),
    }


step_length = 0.1
grad_weight = 0.01
cubic_weight = 1.0
couple_weight = 0.5
screening = 0.0001
damping = 2.0 / 3.0
field_values = (0.8 * math.sin(0.6 * math.pi), 0.8 * math.sin(0.8 * math.pi))


def level_diagonal(grid_level):
    return 2.0 * 0.25 ** grid_level + screening


def stencil(iterate, beneath, overhead, grid_level):
    return (2.0 * iterate - beneath - overhead) * (0.25 ** grid_level) + screening * iterate


def plain_cycle(source, grid_level):
    diagonal = level_diagonal(grid_level)
    if source.shape[1] == 1:
        return source / diagonal

    def apply_plain(iterate):
        padded = jnp.pad(iterate, ((0, 0), (1, 1), (0, 0)))
        return stencil(iterate, padded[:, :-2], padded[:, 2:], grid_level)

    correction = damping * source / diagonal
    residual = source - apply_plain(correction)
    coarse = (residual[:, 0::2] + residual[:, 1::2]) * 0.5
    correction = correction + jnp.repeat(plain_cycle(coarse, grid_level + 1), 2, axis=1)
    return correction + damping * (source - apply_plain(correction)) / diagonal


def planar_stencil(current, south_rim, north_rim, west_rim, east_rim):
    column = jnp.arange(128) % 16
    south_value = jnp.concatenate([south_rim, current[..., :-16]], axis=-1)
    north_value = jnp.concatenate([current[..., 16:], north_rim], axis=-1)
    west_value = jnp.where(column == 0, jnp.repeat(west_rim, 16, axis=-1),
                           jnp.concatenate([current[..., :1], current[..., :-1]], axis=-1))
    east_value = jnp.where(column == 15, jnp.repeat(east_rim, 16, axis=-1),
                           jnp.concatenate([current[..., 1:], current[..., -1:]], axis=-1))
    return south_value + north_value + west_value + east_value - 4.0 * current


def advance(current, quadratic, neighbours, factor, field_value):
    extended = jnp.pad(current, ((0, 0), (0, 0), (1, 1), (0, 0)), mode="edge")
    beneath = extended[:, :, :-2]
    overhead = extended[:, :, 2:]
    vertical = beneath + overhead - 2.0 * current
    charge = -(overhead[2] - beneath[2]) * 0.5
    potential = plain_cycle(charge, 0)
    rimmed = jnp.pad(potential, ((0, 0), (1, 1), (0, 0)))
    depolarizing = -(rimmed[:, 2:] - rimmed[:, :-2]) * 0.5
    south_rim = jnp.take(current[..., 112:], neighbours[0], axis=1)
    north_rim = jnp.take(current[..., :16], neighbours[1], axis=1)
    west_rim = jnp.take(current[..., 15::16], neighbours[2], axis=1)
    east_rim = jnp.take(current[..., 0::16], neighbours[3], axis=1)
    planar = planar_stencil(current, south_rim, north_rim, west_rim, east_rim)
    square = current[0] * current[0] + current[1] * current[1] + current[2] * current[2]
    response = quadratic[None] * current + cubic_weight * current * current * current \
        + couple_weight * current * (square[None] - current * current)
    response = jnp.concatenate([response[:2], response[2:] - (field_value + depolarizing)[None]], axis=0)
    updated = current - step_length * response + grad_weight * (factor * planar + vertical)
    return updated, depolarizing


def reference(polarization, quadratic, neighbours, refinement):
    factor = (jnp.where(refinement >= 1, 4.0, 1.0) * jnp.where(refinement >= 2, 4.0, 1.0)).astype(polarization.dtype)
    factor = factor[None, :, None, None]
    current = polarization
    depolarizing = jnp.zeros_like(quadratic)
    for field_value in field_values:
        current, depolarizing = advance(current, quadratic, neighbours, factor, field_value)
    return current, depolarizing
```

```python
import functools
import math

import jax
import jax.numpy as jnp
import numpy as np
from jax import lax
from jax.experimental import pallas as pl
from jax.experimental.pallas import tpu as pltpu
from jax.sharding import PartitionSpec as P

step_length = 0.1
grad_weight = 0.01
couple_weight = 0.5
screening = 0.0001
damping = 2.0 / 3.0
field_values = (0.8 * math.sin(0.6 * math.pi), 0.8 * math.sin(0.8 * math.pi))

MESH = pl.DeviceIdType.MESH
HIGHEST = lax.Precision.HIGHEST

CELLS = 64
COUNT = 16
NEAR = 13
FAR = 3
SLOT = 16
SENT = 40
HEARD = 72

PARTNERS = sorted(
    [(dx, dy) for dx in range(4) for dy in range(4) if dx or dy],
    key=lambda d: -(min(d[0], 4 - d[0]) + min(d[1], 4 - d[1])),
)
FARTHER = sorted(range(2, 15), key=lambda o: -min(o, 16 - o))


def column_cycle(source, level):
    diagonal = 2.0 * 0.25**level + screening
    if source.shape[0] == 1:
        return source / diagonal

    def apply(v):
        padded = np.pad(v, ((1, 1), (0, 0)))
        return (2.0 * v - padded[:-2] - padded[2:]) * 0.25**level + screening * v

    correction = damping * source / diagonal
    residual = source - apply(correction)
    coarse = (residual[0::2] + residual[1::2]) * 0.5
    correction = correction + np.repeat(column_cycle(coarse, level + 1), 2, axis=0)
    return correction + damping * (source - apply(correction)) / diagonal


def field_operator(cells):
    padded = np.pad(np.eye(cells), ((1, 1), (0, 0)), mode="edge")
    charge = -(padded[2:] - padded[:-2]) * 0.5
    rimmed = np.pad(column_cycle(charge, 0), ((1, 1), (0, 0)))
    return -(rimmed[2:] - rimmed[:-2]) * 0.5


def row_basis(block, rank):
    rest = block.copy()
    rows = np.zeros((rank, block.shape[1]))
    for k in range(rank):
        norms = np.sum(rest * rest, axis=1)
        best = int(np.argmax(norms))
        if norms[best] < 1e-24:
            break
        row = rest[best]
        for _ in range(2):
            for earlier in rows[:k]:
                row = row - np.sum(row * earlier) * earlier
        row = row / np.sqrt(np.sum(row * row))
        rows[k] = row
        rest = rest - np.sum(rest * row, axis=1, keepdims=True) * row
    return rows


def project(block, rows):
    return np.stack([np.sum(block * row, axis=1) for row in rows], axis=1)


@functools.cache
def layer_constants():
    whole = field_operator(CELLS * COUNT)

    def block(d, e):
        return whole[d * CELLS : (d + 1) * CELLS, e * CELLS : (e + 1) * CELLS]

    table = np.zeros((COUNT, SENT + CELLS + CELLS, 128))
    for e in range(COUNT):
        table[e, SENT : SENT + CELLS, :CELLS] = block(e, e)
        far = np.concatenate([block(d, e) for d in range(COUNT) if abs(d - e) > 1])
        basis = row_basis(far, FAR)
        table[e, 2 * SLOT : 2 * SLOT + FAR, :CELLS] = basis
        for o in range(2, COUNT - 1):
            d = (e - o) % COUNT
            first = 2 * SLOT + FAR * (o - 2)
            if abs(d - e) > 1:
                table[d, SENT + CELLS :, first : first + FAR] = project(block(d, e), basis)
        for first, d in ((0, (e + 1) % COUNT), (SLOT, (e - 1) % COUNT)):
            basis = row_basis(block(d, e), NEAR)
            table[e, first : first + NEAR, :CELLS] = basis
            table[d, SENT + CELLS :, first : first + NEAR] = project(block(d, e), basis)
    return table.astype(np.float32)


def kernel(
    pol, quad, nbr_s, nbr_v, refine, consts,
    out, dep_out,
    cur, nxt, qv, cv, dep, mine, faces0, faces1, ssend, lsend, lrecv, tab_v, tab_s,
    ps, pr, ls, lr, local,
):
    faces = (faces0, faces1)
    me = lax.axis_index("patch")
    my = lax.axis_index("layer")
    mx, my_y = me // 4, lax.rem(me, 4)

    def patch_peer(dx, dy):
        return (lax.rem(mx + dx, 4) * 4 + lax.rem(my_y + dy, 4), my)

    def layer_peer(o):
        return (me, lax.rem(my + o, COUNT))

    barrier = pltpu.get_barrier_semaphore()
    for dx, dy in PARTNERS:
        pl.semaphore_signal(barrier, inc=1, device_id=patch_peer(dx, dy), device_id_type=MESH)
    for o in range(1, COUNT):
        pl.semaphore_signal(barrier, inc=1, device_id=layer_peer(o), device_id_type=MESH)

    fetch_p = pltpu.make_async_copy(pol, cur, local.at[0])
    fetch_c = pltpu.make_async_copy(consts.at[my], cv, local.at[1])
    fetch_q = pltpu.make_async_copy(quad, qv, local.at[2])
    fetch_p.start()
    fetch_c.start()
    fetch_q.start()

    lane = lax.broadcasted_iota(jnp.int32, (8, 128), 1)
    row = lax.broadcasted_iota(jnp.int32, (8, 128), 0)
    block16 = lane // 16
    residue = lax.rem(lane, 16)

    def relative(device):
        return lax.rem(device // 4 - mx + 4, 4) * 4 + lax.rem(lax.rem(device, 4) - my_y + 4, 4)

    face = lax.broadcasted_iota(jnp.int32, (4, 8), 0)
    there = nbr_v[...]
    device = there // 8
    mirrored = face + 1 - 2 * lax.rem(face, 2)
    key = mirrored * 8 + lax.rem(there, 8)
    rank = jnp.zeros((4, 8), jnp.int32)
    least = jnp.zeros((8, 128), jnp.int32)
    most = jnp.zeros((8, 128), jnp.int32)
    for f in range(4):
        for s in range(8):
            n = nbr_s[f, s]
            other_key = (f ^ 1) * 8 + lax.rem(n, 8)
            before = (device == n // 8) & (key > other_key)
            rank = rank + jnp.where(before, 1, 0)
            most = jnp.where(lane == relative(n // 8), f * 8 + s, most)
            n = nbr_s[3 - f, 7 - s]
            least = jnp.where(lane == relative(n // 8), (3 - f) * 8 + 7 - s, least)
    place = jnp.where(
        device == me,
        (jnp.minimum(mirrored, 2) * 8 + lax.rem(there, 8)) * 3,
        72 + (relative(device) - 1) * 6 + jnp.minimum(rank, 1) * 3,
    )
    tab_v[pl.ds(0, 8), :] = jnp.where(least >= 24, least - 8, least) * 3
    tab_v[pl.ds(8, 8), :] = jnp.where(most >= 24, most - 8, most) * 3
    tab_v[pl.ds(16, 4), pl.ds(0, 8)] = place
    to_scalar = pltpu.make_async_copy(tab_v, tab_s, local.at[3])
    to_scalar.start()

    lrecv[0, pl.ds((HEARD - 1) * 8, 8), :] = jnp.zeros((8, 128), jnp.float32)
    lrecv[1, pl.ds((HEARD - 1) * 8, 8), :] = jnp.zeros((8, 128), jnp.float32)

    def rows_of(c, s):
        return pl.multiple_of(c * 512 + s * CELLS, CELLS)

    def prepare(step, s, c, cells):
        high, low, sides = cells[7], cells[7], cells[0]
        for g in range(7):
            turned = pltpu.roll(cells[g], 16 * (g + 1), 1)
            high = jnp.where(block16 == g, turned, high)
            low = jnp.where(block16 == g + 1, turned, low)
        for g in range(1, 8):
            turned = pltpu.roll(cells[g], (30 * g) % 128, 1)
            sides = jnp.where(
                (residue == 16 - 2 * g) | (residue == 15 - 2 * g), turned, sides
            )
        for ref in (mine, faces[step]):
            ref[s * 3 + c] = low
            ref[(8 + s) * 3 + c] = high
            ref[(16 + s) * 3 + c] = sides

    def functionals(step, s, p2, edges):
        got = jnp.dot(
            cv[pl.ds(0, SENT), pl.ds(0, CELLS)], p2,
            precision=HIGHEST, preferred_element_type=jnp.float32,
        )
        lsend[step, pl.ds(s, SENT, stride=8), :] = got
        for c in range(3):
            below, above = edges[c]
            lsend[step, pl.ds((NEAR + c) * 8 + s, 1), :] = above
            lsend[step, pl.ds((SLOT + NEAR + c) * 8 + s, 1), :] = below

    def send(step):
        copies = []
        for o in FARTHER + [1, COUNT - 1]:
            if o == 1:
                source, target, rows = 0, 0, SLOT * 8
            elif o == COUNT - 1:
                source, target, rows = SLOT * 8, SLOT * 8, SLOT * 8
            else:
                source, rows = 2 * SLOT * 8, FAR * 8
                target = (2 * SLOT + FAR * (COUNT - o - 2)) * 8
            copies.append(
                pltpu.make_async_remote_copy(
                    src_ref=lsend.at[step, pl.ds(source, rows), :],
                    dst_ref=lrecv.at[step, pl.ds(target, rows), :],
                    send_sem=ls.at[step, o],
                    recv_sem=lr.at[step, COUNT - o],
                    device_id=layer_peer(o),
                    device_id_type=MESH,
                )
            )
            copies[-1].start()
        for dx, dy in PARTNERS:
            to = dx * 4 + dy
            back = (4 - dx) % 4 * 4 + (4 - dy) % 4
            for c in range(3):
                ssend[step, (to - 1) * 6 + c] = mine[tab_s[0, to] + c]
                ssend[step, (to - 1) * 6 + 3 + c] = mine[tab_s[8, to] + c]
            copies.append(
                pltpu.make_async_remote_copy(
                    src_ref=ssend.at[step, pl.ds((to - 1) * 6, 6)],
                    dst_ref=faces[step].at[pl.ds(72 + (back - 1) * 6, 6)],
                    send_sem=ps.at[step, to],
                    recv_sem=pr.at[step, back],
                    device_id=patch_peer(dx, dy),
                    device_id_type=MESH,
                )
            )
            copies[-1].start()
        return copies

    def tiles(ref, c, s):
        return [ref[pl.ds(rows_of(c, s) + 8 * g, 8), :] for g in range(8)]

    def local_part(step, now, later):
        def body(s, carry):
            level = refine[s]
            factor = jnp.where(level >= 1, 4.0, 1.0) * jnp.where(level >= 2, 4.0, 1.0)
            weight = grad_weight * factor
            cells = [now[pl.ds(rows_of(c, s), CELLS), :] for c in range(3)]
            lanes = lax.broadcasted_iota(jnp.int32, (CELLS, 128), 1)
            depth = lax.broadcasted_iota(jnp.int32, (CELLS, 128), 0)
            column = lax.rem(lanes, 16)
            square = cells[0] * cells[0] + cells[1] * cells[1] + cells[2] * cells[2]
            common = (
                1.0
                - 2.0 * grad_weight
                - 4.0 * weight
                - step_length * qv[pl.ds(pl.multiple_of(s * CELLS, CELLS), CELLS), :]
                - step_length * couple_weight * square
            )
            for c in range(3):
                x = cells[c]
                planar = (
                    jnp.where(lanes >= 16, pltpu.roll(x, 16, 1), 0.0)
                    + jnp.where(lanes < 112, pltpu.roll(x, 112, 1), 0.0)
                    + jnp.where(column > 0, pltpu.roll(x, 1, 1), 0.0)
                    + jnp.where(column < 15, pltpu.roll(x, 127, 1), 0.0)
                )
                vertical = jnp.where(depth > 0, pltpu.roll(x, 1, 0), 0.0) + jnp.where(
                    depth < CELLS - 1, pltpu.roll(x, CELLS - 1, 0), 0.0
                )
                new = (
                    x * (common - step_length * (1.0 - couple_weight) * x * x)
                    + weight * planar
                    + grad_weight * vertical
                )
                if c == 2:
                    new = new + step_length * field_values[step]
                later[pl.ds(rows_of(c, s), CELLS), :] = new
            dep[pl.ds(pl.multiple_of(s * CELLS, CELLS), CELLS), :] = jnp.dot(
                cv[pl.ds(SENT, CELLS), pl.ds(0, CELLS)], cells[2],
                precision=HIGHEST, preferred_element_type=jnp.float32,
            )
            return carry

        lax.fori_loop(0, 8, body, 0)

    def finish(step, now, later, dep_ref, out_ref):
        def body(s, carry):
            level = refine[s]
            factor = jnp.where(level >= 1, 4.0, 1.0) * jnp.where(level >= 2, 4.0, 1.0)
            weight = grad_weight * factor
            south_w = jnp.where(lane < 16, weight, 0.0)
            north_w = jnp.where(lane >= 112, weight, 0.0)
            west_w = jnp.where(residue == 0, weight, 0.0)
            east_w = jnp.where(residue == 15, weight, 0.0)
            heard = lrecv[step, pl.ds(s, HEARD, stride=8), :]
            field = dep[pl.ds(pl.multiple_of(s * CELLS, CELLS), CELLS), :] + jnp.dot(
                cv[pl.ds(SENT + CELLS, CELLS), pl.ds(0, HEARD)], heard,
                precision=HIGHEST, preferred_element_type=jnp.float32,
            )
            if dep_ref is not None:
                dep_ref[pl.ds(pl.multiple_of(s * CELLS, CELLS), CELLS), :] = field
            edges = []
            for c in range(3):
                x = tiles(later, c, s)
                south = faces[step][tab_s[16, s] + c]
                north = faces[step][tab_s[17, s] + c]
                west = faces[step][tab_s[18, s] + c]
                east = faces[step][tab_s[19, s] + c]
                turned = [
                    pltpu.roll(jnp.where(block16 == k, south, north), (128 - 16 * k) % 128, 1)
                    for k in range(8)
                ]
                mixed = jnp.where(lax.rem(lane, 2) == 1, west, east)
                sides = [pltpu.roll(mixed, (-15 - 30 * k) % 128, 1) for k in range(-1, 8)]
                for g in range(8):
                    x[g] = (
                        x[g]
                        + south_w * turned[g]
                        + north_w * turned[(g + 2) % 8]
                        + west_w * sides[g + 1]
                        + east_w * sides[g]
                    )
                below = jnp.where(
                    my == 0,
                    now[pl.ds(rows_of(c, s), 1), :],
                    lrecv[step, pl.ds((NEAR + c) * 8 + s, 1), :],
                )
                above = jnp.where(
                    my == COUNT - 1,
                    now[pl.ds(rows_of(c, s) + CELLS - 1, 1), :],
                    lrecv[step, pl.ds((SLOT + NEAR + c) * 8 + s, 1), :],
                )
                x[0] = x[0] + jnp.where(row == 0, grad_weight * below, 0.0)
                x[7] = x[7] + jnp.where(row == 7, grad_weight * above, 0.0)
                if c == 2:
                    x = [x[g] + step_length * field[8 * g : 8 * g + 8] for g in range(8)]
                for g in range(8):
                    out_ref[pl.ds(rows_of(c, s) + 8 * g, 8), :] = x[g]
                if out_ref is not out:
                    prepare(step + 1, s, c, x)
                    edges.append((x[0][0:1], x[7][7:8]))
                    if c == 2:
                        functionals(step + 1, s, jnp.concatenate(x, axis=0), edges)
            return carry

        lax.fori_loop(0, 8, body, 0)

    fetch_p.wait()
    fetch_c.wait()

    def first(s, carry):
        edges = []
        for c in range(3):
            x = tiles(cur, c, s)
            prepare(0, s, c, x)
            edges.append((x[0][0:1], x[7][7:8]))
            if c == 2:
                functionals(0, s, jnp.concatenate(x, axis=0), edges)
        return carry

    lax.fori_loop(0, 8, first, 0)
    to_scalar.wait()
    pl.semaphore_wait(barrier, 2 * (COUNT - 1))
    copies = send(0)
    fetch_q.wait()
    local_part(0, cur, nxt)
    for copy in copies:
        copy.wait_recv()
    finish(0, cur, nxt, None, nxt)
    more = send(1)
    local_part(1, nxt, cur)
    for copy in more:
        copy.wait_recv()
    finish(1, nxt, cur, dep_out, out)
    for copy in copies + more:
        copy.wait_send()


def on_device(polarization, quadratic, neighbours, refinement):
    vmem = pl.BlockSpec(memory_space=pltpu.VMEM)
    smem = pl.BlockSpec(memory_space=pltpu.SMEM)
    hbm = pl.BlockSpec(memory_space=pl.ANY)
    dma = pltpu.SemaphoreType.DMA
    f32 = jnp.float32
    final, field = pl.pallas_call(
        kernel,
        out_shape=(
            jax.ShapeDtypeStruct((1536, 128), f32),
            jax.ShapeDtypeStruct((512, 128), f32),
        ),
        in_specs=[hbm, hbm, smem, vmem, smem, hbm],
        out_specs=(vmem, vmem),
        scratch_shapes=[
            pltpu.VMEM((1536, 128), f32),
            pltpu.VMEM((1536, 128), f32),
            pltpu.VMEM((512, 128), f32),
            pltpu.VMEM((SENT + 2 * CELLS, 128), f32),
            pltpu.VMEM((512, 128), f32),
            pltpu.VMEM((72, 8, 128), f32),
            pltpu.VMEM((72 + 90, 8, 128), f32),
            pltpu.VMEM((72 + 90, 8, 128), f32),
            pltpu.VMEM((2, 90, 8, 128), f32),
            pltpu.VMEM((2, SENT * 8, 128), f32),
            pltpu.VMEM((2, HEARD * 8, 128), f32),
            pltpu.VMEM((24, 128), jnp.int32),
            pltpu.SMEM((24, 128), jnp.int32),
            dma((2, 16)),
            dma((2, 16)),
            dma((2, 16)),
            dma((2, 16)),
            dma((4,)),
        ],
        compiler_params=pltpu.CompilerParams(
            collective_id=0, has_side_effects=True, vmem_limit_bytes=32 << 20
        ),
    )(
        polarization.reshape(1536, 128),
        quadratic.reshape(512, 128),
        neighbours,
        neighbours,
        refinement,
        jnp.asarray(layer_constants()),
    )
    return final.reshape(polarization.shape), field.reshape(quadratic.shape)


def solution(mesh):
    in_specs = (
        P(None, "patch", "layer", None),
        P("patch", "layer", None),
        P(None, "patch"),
        P("patch"),
    )
    out_specs = (P(None, "patch", "layer", None), P("patch", "layer", None))
    return jax.shard_map(
        on_device, mesh=mesh, in_specs=in_specs, out_specs=out_specs, check_vma=False
    )
```

```python
import functools
import math

import jax
import jax.numpy as jnp
import numpy as np
from jax import lax
from jax.experimental import pallas as pl
from jax.experimental.pallas import tpu as pltpu
from jax.sharding import PartitionSpec as P

step_length = 0.1
grad_weight = 0.01
couple_weight = 0.5
screening = 0.0001
damping = 2.0 / 3.0
field_values = (0.8 * math.sin(0.6 * math.pi), 0.8 * math.sin(0.8 * math.pi))

MESH = pl.DeviceIdType.MESH
HIGHEST = lax.Precision.HIGHEST

CELLS = 64
COUNT = 16
NEAR = 13
FAR = 3
SLOT = 16
SENT = 40
HEARD = 72

PARTNERS = sorted(
    [(dx, dy) for dx in range(4) for dy in range(4) if dx or dy],
    key=lambda d: -(min(d[0], 4 - d[0]) + min(d[1], 4 - d[1])),
)
FARTHER = sorted(range(2, 15), key=lambda o: -min(o, 16 - o))


def column_cycle(source, level):
    diagonal = 2.0 * 0.25**level + screening
    if source.shape[0] == 1:
        return source / diagonal

    def apply(v):
        padded = np.pad(v, ((1, 1), (0, 0)))
        return (2.0 * v - padded[:-2] - padded[2:]) * 0.25**level + screening * v

    correction = damping * source / diagonal
    residual = source - apply(correction)
    coarse = (residual[0::2] + residual[1::2]) * 0.5
    correction = correction + np.repeat(column_cycle(coarse, level + 1), 2, axis=0)
    return correction + damping * (source - apply(correction)) / diagonal


def field_operator(cells):
    padded = np.pad(np.eye(cells), ((1, 1), (0, 0)), mode="edge")
    charge = -(padded[2:] - padded[:-2]) * 0.5
    rimmed = np.pad(column_cycle(charge, 0), ((1, 1), (0, 0)))
    return -(rimmed[2:] - rimmed[:-2]) * 0.5


def row_basis(block, rank):
    rest = block.copy()
    rows = np.zeros((rank, block.shape[1]))
    for k in range(rank):
        norms = np.sum(rest * rest, axis=1)
        best = int(np.argmax(norms))
        if norms[best] < 1e-24:
            break
        row = rest[best]
        for _ in range(2):
            for earlier in rows[:k]:
                row = row - np.sum(row * earlier) * earlier
        row = row / np.sqrt(np.sum(row * row))
        rows[k] = row
        rest = rest - np.sum(rest * row, axis=1, keepdims=True) * row
    return rows


def project(block, rows):
    return np.stack([np.sum(block * row, axis=1) for row in rows], axis=1)


@functools.cache
def layer_constants():
    whole = field_operator(CELLS * COUNT)

    def block(d, e):
        return whole[d * CELLS : (d + 1) * CELLS, e * CELLS : (e + 1) * CELLS]

    table = np.zeros((COUNT, SENT + CELLS + CELLS, 128))
    for e in range(COUNT):
        table[e, SENT : SENT + CELLS, :CELLS] = block(e, e)
        far = np.concatenate([block(d, e) for d in range(COUNT) if abs(d - e) > 1])
        basis = row_basis(far, FAR)
        table[e, 2 * SLOT : 2 * SLOT + FAR, :CELLS] = basis
        for o in range(2, COUNT - 1):
            d = (e - o) % COUNT
            first = 2 * SLOT + FAR * (o - 2)
            if abs(d - e) > 1:
                table[d, SENT + CELLS :, first : first + FAR] = project(block(d, e), basis)
        for first, d in ((0, (e + 1) % COUNT), (SLOT, (e - 1) % COUNT)):
            basis = row_basis(block(d, e), NEAR)
            table[e, first : first + NEAR, :CELLS] = basis
            table[d, SENT + CELLS :, first : first + NEAR] = project(block(d, e), basis)
    return table.astype(np.float32)


def kernel(
    pol, quad, nbr, levels, consts,
    out, dep_out,
    nbr_s, nbr_v, refine, cur, nxt, qv, cv, dep, mine, faces0, faces1, ssend, lsend, lrecv, tab_v, tab_s,
    ps, pr, ls, lr, local,
):
    faces = (faces0, faces1)
    me = lax.axis_index("patch")
    my = lax.axis_index("layer")
    mx, my_y = me // 4, lax.rem(me, 4)

    def patch_peer(dx, dy):
        return (lax.rem(mx + dx, 4) * 4 + lax.rem(my_y + dy, 4), my)

    def layer_peer(o):
        return (me, lax.rem(my + o, COUNT))

    barrier = pltpu.get_barrier_semaphore()
    for dx, dy in PARTNERS:
        pl.semaphore_signal(barrier, inc=1, device_id=patch_peer(dx, dy), device_id_type=MESH)
    for o in range(1, COUNT):
        pl.semaphore_signal(barrier, inc=1, device_id=layer_peer(o), device_id_type=MESH)

    fetch_p = pltpu.make_async_copy(pol, cur, local.at[0])
    fetch_c = pltpu.make_async_copy(consts.at[my], cv, local.at[1])
    fetch_q = pltpu.make_async_copy(quad, qv, local.at[2])
    fetch_n = pltpu.make_async_copy(nbr, nbr_s, local.at[4])
    fetch_v = pltpu.make_async_copy(nbr, nbr_v, local.at[5])
    fetch_l = pltpu.make_async_copy(levels, refine, local.at[6])
    fetch_n.start()
    fetch_v.start()
    fetch_p.start()
    fetch_c.start()
    fetch_l.start()
    fetch_q.start()

    lane = lax.broadcasted_iota(jnp.int32, (8, 128), 1)
    row = lax.broadcasted_iota(jnp.int32, (8, 128), 0)
    block16 = lane // 16
    residue = lax.rem(lane, 16)

    def relative(device):
        return lax.rem(device // 4 - mx + 4, 4) * 4 + lax.rem(lax.rem(device, 4) - my_y + 4, 4)

    fetch_n.wait()
    fetch_v.wait()
    face = lax.broadcasted_iota(jnp.int32, (4, 8), 0)
    there = nbr_v[...]
    device = there // 8
    mirrored = face + 1 - 2 * lax.rem(face, 2)
    key = mirrored * 8 + lax.rem(there, 8)
    rank = jnp.zeros((4, 8), jnp.int32)
    least = jnp.zeros((8, 128), jnp.int32)
    most = jnp.zeros((8, 128), jnp.int32)
    for f in range(4):
        for s in range(8):
            n = nbr_s[f, s]
            other_key = (f ^ 1) * 8 + lax.rem(n, 8)
            before = (device == n // 8) & (key > other_key)
            rank = rank + jnp.where(before, 1, 0)
            most = jnp.where(lane == relative(n // 8), f * 8 + s, most)
            n = nbr_s[3 - f, 7 - s]
            least = jnp.where(lane == relative(n // 8), (3 - f) * 8 + 7 - s, least)
    place = jnp.where(
        device == me,
        (jnp.minimum(mirrored, 2) * 8 + lax.rem(there, 8)) * 3,
        72 + (relative(device) - 1) * 6 + jnp.minimum(rank, 1) * 3,
    )
    tab_v[pl.ds(0, 8), :] = jnp.where(least >= 24, least - 8, least) * 3
    tab_v[pl.ds(8, 8), :] = jnp.where(most >= 24, most - 8, most) * 3
    tab_v[pl.ds(16, 4), pl.ds(0, 8)] = place
    to_scalar = pltpu.make_async_copy(tab_v, tab_s, local.at[3])
    to_scalar.start()

    lrecv[0, pl.ds((HEARD - 1) * 8, 8), :] = jnp.zeros((8, 128), jnp.float32)
    lrecv[1, pl.ds((HEARD - 1) * 8, 8), :] = jnp.zeros((8, 128), jnp.float32)

    def rows_of(c, s):
        return pl.multiple_of(c * 512 + s * CELLS, CELLS)

    def prepare(step, s, c, cells):
        high, low, sides = cells[7], cells[7], cells[0]
        for g in range(7):
            turned = pltpu.roll(cells[g], 16 * (g + 1), 1)
            high = jnp.where(block16 == g, turned, high)
            low = jnp.where(block16 == g + 1, turned, low)
        for g in range(1, 8):
            turned = pltpu.roll(cells[g], (30 * g) % 128, 1)
            sides = jnp.where(
                (residue == 16 - 2 * g) | (residue == 15 - 2 * g), turned, sides
            )
        for ref in (mine, faces[step]):
            ref[s * 3 + c] = low
            ref[(8 + s) * 3 + c] = high
            ref[(16 + s) * 3 + c] = sides

    def functionals(step, s, p2, edges):
        got = jnp.dot(
            cv[pl.ds(0, SENT), pl.ds(0, CELLS)], p2,
            precision=HIGHEST, preferred_element_type=jnp.float32,
        )
        lsend[step, pl.ds(s, SENT, stride=8), :] = got
        for c in range(3):
            below, above = edges[c]
            lsend[step, pl.ds((NEAR + c) * 8 + s, 1), :] = above
            lsend[step, pl.ds((SLOT + NEAR + c) * 8 + s, 1), :] = below

    def send(step):
        copies = []
        for o in FARTHER + [1, COUNT - 1]:
            if o == 1:
                source, target, rows = 0, 0, SLOT * 8
            elif o == COUNT - 1:
                source, target, rows = SLOT * 8, SLOT * 8, SLOT * 8
            else:
                source, rows = 2 * SLOT * 8, FAR * 8
                target = (2 * SLOT + FAR * (COUNT - o - 2)) * 8
            copies.append(
                pltpu.make_async_remote_copy(
                    src_ref=lsend.at[step, pl.ds(source, rows), :],
                    dst_ref=lrecv.at[step, pl.ds(target, rows), :],
                    send_sem=ls.at[step, o],
                    recv_sem=lr.at[step, COUNT - o],
                    device_id=layer_peer(o),
                    device_id_type=MESH,
                )
            )
            copies[-1].start()
        for dx, dy in PARTNERS:
            to = dx * 4 + dy
            back = (4 - dx) % 4 * 4 + (4 - dy) % 4
            for c in range(3):
                ssend[step, (to - 1) * 6 + c] = mine[tab_s[0, to] + c]
                ssend[step, (to - 1) * 6 + 3 + c] = mine[tab_s[8, to] + c]
            copies.append(
                pltpu.make_async_remote_copy(
                    src_ref=ssend.at[step, pl.ds((to - 1) * 6, 6)],
                    dst_ref=faces[step].at[pl.ds(72 + (back - 1) * 6, 6)],
                    send_sem=ps.at[step, to],
                    recv_sem=pr.at[step, back],
                    device_id=patch_peer(dx, dy),
                    device_id_type=MESH,
                )
            )
            copies[-1].start()
        return copies

    def tiles(ref, c, s):
        return [ref[pl.ds(rows_of(c, s) + 8 * g, 8), :] for g in range(8)]

    def local_part(step, now, later):
        def body(s, carry):
            level = refine[s]
            factor = jnp.where(level >= 1, 4.0, 1.0) * jnp.where(level >= 2, 4.0, 1.0)
            weight = grad_weight * factor
            cells = [now[pl.ds(rows_of(c, s), CELLS), :] for c in range(3)]
            lanes = lax.broadcasted_iota(jnp.int32, (CELLS, 128), 1)
            depth = lax.broadcasted_iota(jnp.int32, (CELLS, 128), 0)
            column = lax.rem(lanes, 16)
            square = cells[0] * cells[0] + cells[1] * cells[1] + cells[2] * cells[2]
            common = (
                1.0
                - 2.0 * grad_weight
                - 4.0 * weight
                - step_length * qv[pl.ds(pl.multiple_of(s * CELLS, CELLS), CELLS), :]
                - step_length * couple_weight * square
            )
            for c in range(3):
                x = cells[c]
                planar = (
                    jnp.where(lanes >= 16, pltpu.roll(x, 16, 1), 0.0)
                    + jnp.where(lanes < 112, pltpu.roll(x, 112, 1), 0.0)
                    + jnp.where(column > 0, pltpu.roll(x, 1, 1), 0.0)
                    + jnp.where(column < 15, pltpu.roll(x, 127, 1), 0.0)
                )
                vertical = jnp.where(depth > 0, pltpu.roll(x, 1, 0), 0.0) + jnp.where(
                    depth < CELLS - 1, pltpu.roll(x, CELLS - 1, 0), 0.0
                )
                new = (
                    x * (common - step_length * (1.0 - couple_weight) * x * x)
                    + weight * planar
                    + grad_weight * vertical
                )
                if c == 2:
                    new = new + step_length * field_values[step]
                later[pl.ds(rows_of(c, s), CELLS), :] = new
            dep[pl.ds(pl.multiple_of(s * CELLS, CELLS), CELLS), :] = jnp.dot(
                cv[pl.ds(SENT, CELLS), pl.ds(0, CELLS)], cells[2],
                precision=HIGHEST, preferred_element_type=jnp.float32,
            )
            return carry

        lax.fori_loop(0, 8, body, 0)

    def finish(step, now, later, dep_ref, out_ref):
        def body(s, carry):
            level = refine[s]
            factor = jnp.where(level >= 1, 4.0, 1.0) * jnp.where(level >= 2, 4.0, 1.0)
            weight = grad_weight * factor
            south_w = jnp.where(lane < 16, weight, 0.0)
            north_w = jnp.where(lane >= 112, weight, 0.0)
            west_w = jnp.where(residue == 0, weight, 0.0)
            east_w = jnp.where(residue == 15, weight, 0.0)
            heard = lrecv[step, pl.ds(s, HEARD, stride=8), :]
            field = dep[pl.ds(pl.multiple_of(s * CELLS, CELLS), CELLS), :] + jnp.dot(
                cv[pl.ds(SENT + CELLS, CELLS), pl.ds(0, HEARD)], heard,
                precision=HIGHEST, preferred_element_type=jnp.float32,
            )
            if dep_ref is not None:
                dep_ref[pl.ds(pl.multiple_of(s * CELLS, CELLS), CELLS), :] = field
            edges = []
            for c in range(3):
                x = tiles(later, c, s)
                south = faces[step][tab_s[16, s] + c]
                north = faces[step][tab_s[17, s] + c]
                west = faces[step][tab_s[18, s] + c]
                east = faces[step][tab_s[19, s] + c]
                turned = [
                    pltpu.roll(jnp.where(block16 == k, south, north), (128 - 16 * k) % 128, 1)
                    for k in range(8)
                ]
                mixed = jnp.where(lax.rem(lane, 2) == 1, west, east)
                sides = [pltpu.roll(mixed, (-15 - 30 * k) % 128, 1) for k in range(-1, 8)]
                for g in range(8):
                    x[g] = (
                        x[g]
                        + south_w * turned[g]
                        + north_w * turned[(g + 2) % 8]
                        + west_w * sides[g + 1]
                        + east_w * sides[g]
                    )
                below = jnp.where(
                    my == 0,
                    now[pl.ds(rows_of(c, s), 1), :],
                    lrecv[step, pl.ds((NEAR + c) * 8 + s, 1), :],
                )
                above = jnp.where(
                    my == COUNT - 1,
                    now[pl.ds(rows_of(c, s) + CELLS - 1, 1), :],
                    lrecv[step, pl.ds((SLOT + NEAR + c) * 8 + s, 1), :],
                )
                x[0] = x[0] + jnp.where(row == 0, grad_weight * below, 0.0)
                x[7] = x[7] + jnp.where(row == 7, grad_weight * above, 0.0)
                if c == 2:
                    x = [x[g] + step_length * field[8 * g : 8 * g + 8] for g in range(8)]
                for g in range(8):
                    out_ref[pl.ds(rows_of(c, s) + 8 * g, 8), :] = x[g]
                if out_ref is not out:
                    prepare(step + 1, s, c, x)
                    edges.append((x[0][0:1], x[7][7:8]))
                    if c == 2:
                        functionals(step + 1, s, jnp.concatenate(x, axis=0), edges)
            return carry

        lax.fori_loop(0, 8, body, 0)

    fetch_p.wait()
    fetch_c.wait()

    def first(s, carry):
        edges = []
        for c in range(3):
            x = tiles(cur, c, s)
            prepare(0, s, c, x)
            edges.append((x[0][0:1], x[7][7:8]))
            if c == 2:
                functionals(0, s, jnp.concatenate(x, axis=0), edges)
        return carry

    lax.fori_loop(0, 8, first, 0)
    to_scalar.wait()
    pl.semaphore_wait(barrier, 2 * (COUNT - 1))
    copies = send(0)
    fetch_q.wait()
    fetch_l.wait()
    local_part(0, cur, nxt)
    for copy in copies:
        copy.wait_recv()
    finish(0, cur, nxt, None, nxt)
    more = send(1)
    local_part(1, nxt, cur)
    for copy in more:
        copy.wait_recv()
    finish(1, nxt, cur, dep_out, out)
    for copy in copies + more:
        copy.wait_send()


def on_device(polarization, quadratic, neighbours, refinement):
    vmem = pl.BlockSpec(memory_space=pltpu.VMEM)
    hbm = pl.BlockSpec(memory_space=pltpu.HBM)
    dma = pltpu.SemaphoreType.DMA
    f32 = jnp.float32
    final, field = pl.pallas_call(
        kernel,
        out_shape=(
            pltpu.VMEM((1536, 128), f32),
            pltpu.VMEM((512, 128), f32),
        ),
        in_specs=[hbm] * 5,
        out_specs=(vmem, vmem),
        scratch_shapes=[
            pltpu.SMEM((4, 8), jnp.int32),
            pltpu.VMEM((4, 8), jnp.int32),
            pltpu.SMEM((8,), jnp.int32),
            pltpu.VMEM((1536, 128), f32),
            pltpu.VMEM((1536, 128), f32),
            pltpu.VMEM((512, 128), f32),
            pltpu.VMEM((SENT + 2 * CELLS, 128), f32),
            pltpu.VMEM((512, 128), f32),
            pltpu.VMEM((72, 8, 128), f32),
            pltpu.VMEM((72 + 90, 8, 128), f32),
            pltpu.VMEM((72 + 90, 8, 128), f32),
            pltpu.VMEM((2, 90, 8, 128), f32),
            pltpu.VMEM((2, SENT * 8, 128), f32),
            pltpu.VMEM((2, HEARD * 8, 128), f32),
            pltpu.VMEM((24, 128), jnp.int32),
            pltpu.SMEM((24, 128), jnp.int32),
            dma((2, 16)),
            dma((2, 16)),
            dma((2, 16)),
            dma((2, 16)),
            dma((7,)),
        ],
        compiler_params=pltpu.CompilerParams(
            collective_id=0, has_side_effects=True, vmem_limit_bytes=32 << 20
        ),
    )(
        *(
            pltpu.with_memory_space_constraint(x, pltpu.HBM)
            for x in (
                polarization.reshape(1536, 128),
                quadratic.reshape(512, 128),
                neighbours,
                refinement,
                jnp.asarray(layer_constants()),
            )
        )
    )
    return final.reshape(polarization.shape), field.reshape(quadratic.shape)


def solution(mesh):
    in_specs = (
        P(None, "patch", "layer", None),
        P("patch", "layer", None),
        P(None, "patch"),
        P("patch"),
    )
    out_specs = (P(None, "patch", "layer", None), P("patch", "layer", None))
    return jax.shard_map(
        on_device, mesh=mesh, in_specs=in_specs, out_specs=out_specs, check_vma=False
    )
```

```python
import functools
import math

import jax
import jax.numpy as jnp
import numpy as np
from jax import lax
from jax.experimental import pallas as pl
from jax.experimental.pallas import tpu as pltpu
from jax.sharding import PartitionSpec as P

step_length = 0.1
grad_weight = 0.01
couple_weight = 0.5
screening = 0.0001
damping = 2.0 / 3.0
field_values = (0.8 * math.sin(0.6 * math.pi), 0.8 * math.sin(0.8 * math.pi))

MESH = pl.DeviceIdType.MESH
HIGHEST = lax.Precision.HIGHEST

CELLS = 64
COUNT = 16
NEAR = 13
SLOT = 16
ROWS = 64
OWN = 24

PARTNERS = sorted(
    [(dx, dy) for dx in range(4) for dy in range(4) if dx or dy],
    key=lambda d: -(min(d[0], 4 - d[0]) + min(d[1], 4 - d[1])),
)
MESSAGES = {1: (0, NEAR), COUNT - 1: (SLOT, NEAR), 2: (2 * SLOT, 3), COUNT - 2: (2 * SLOT + 3, 3)}
MESSAGES.update({o: (2 * SLOT + 2 * o, 2) for o in range(3, COUNT - 2)})
FARTHER = sorted(range(2, COUNT - 1), key=lambda o: -min(o, COUNT - o))


def column_cycle(source, level):
    diagonal = 2.0 * 0.25**level + screening
    if source.shape[0] == 1:
        return source / diagonal

    def apply(v):
        padded = np.pad(v, ((1, 1), (0, 0)))
        return (2.0 * v - padded[:-2] - padded[2:]) * 0.25**level + screening * v

    correction = damping * source / diagonal
    residual = source - apply(correction)
    coarse = (residual[0::2] + residual[1::2]) * 0.5
    correction = correction + np.repeat(column_cycle(coarse, level + 1), 2, axis=0)
    return correction + damping * (source - apply(correction)) / diagonal


def field_operator(cells):
    padded = np.pad(np.eye(cells), ((1, 1), (0, 0)), mode="edge")
    charge = -(padded[2:] - padded[:-2]) * 0.5
    rimmed = np.pad(column_cycle(charge, 0), ((1, 1), (0, 0)))
    return -(rimmed[2:] - rimmed[:-2]) * 0.5


def row_basis(block, rank):
    rest = block.copy()
    rows = np.zeros((rank, block.shape[1]))
    for k in range(rank):
        norms = np.sum(rest * rest, axis=1)
        best = int(np.argmax(norms))
        if norms[best] < 1e-24:
            break
        row = rest[best]
        for _ in range(2):
            for earlier in rows[:k]:
                row = row - np.sum(row * earlier) * earlier
        row = row / np.sqrt(np.sum(row * row))
        rows[k] = row
        rest = rest - np.sum(rest * row, axis=1, keepdims=True) * row
    return rows


def project(block, rows):
    return np.stack([np.sum(block * row, axis=1) for row in rows], axis=1)


@functools.cache
def layer_constants():
    whole = field_operator(CELLS * COUNT)

    def block(d, e):
        return whole[d * CELLS : (d + 1) * CELLS, e * CELLS : (e + 1) * CELLS]

    table = np.zeros((COUNT, 3 * CELLS, 128))
    for e in range(COUNT):
        table[e, ROWS : ROWS + CELLS, :CELLS] = block(e, e)
        for o, (first, rank) in MESSAGES.items():
            d = (e + o) % COUNT
            basis = row_basis(block(d, e), rank)
            table[e, first : first + rank, :CELLS] = basis
            table[d, ROWS + CELLS :, first : first + rank] = project(block(d, e), basis)
    return table.astype(np.float32)


def product(left, right):
    return jnp.dot(left, right, precision=HIGHEST, preferred_element_type=jnp.float32)


def kernel(
    pol, quad, nbr, levels, consts,
    out, dep_out,
    nbr_s, nbr_v, refine, cur, nxt, qv, cv, dep, mine,
    faces00, faces01, faces02, faces10, faces11, faces12,
    ssend, lsend, lrecv, tab_v, tab_s, ps, pr, ls, lr, local,
):
    faces = ((faces00, faces01, faces02), (faces10, faces11, faces12))
    me = lax.axis_index("patch")
    my = lax.axis_index("layer")
    mx, my_y = me // 4, lax.rem(me, 4)

    def patch_peer(dx, dy):
        return (lax.rem(mx + dx, 4) * 4 + lax.rem(my_y + dy, 4), my)

    def layer_peer(o):
        return (me, lax.rem(my + o, COUNT))

    barrier = pltpu.get_barrier_semaphore()
    for dx, dy in PARTNERS:
        pl.semaphore_signal(barrier, inc=1, device_id=patch_peer(dx, dy), device_id_type=MESH)
    for o in range(1, COUNT):
        pl.semaphore_signal(barrier, inc=1, device_id=layer_peer(o), device_id_type=MESH)

    fetch_p = pltpu.make_async_copy(pol, cur, local.at[0])
    fetch_c = pltpu.make_async_copy(consts.at[my], cv, local.at[1])
    fetch_q = pltpu.make_async_copy(quad, qv, local.at[2])
    fetch_n = pltpu.make_async_copy(nbr, nbr_s, local.at[4])
    fetch_v = pltpu.make_async_copy(nbr, nbr_v, local.at[5])
    fetch_l = pltpu.make_async_copy(levels, refine, local.at[6])
    fetch_n.start()
    fetch_v.start()
    fetch_p.start()
    fetch_c.start()
    fetch_l.start()
    fetch_q.start()

    lane = lax.broadcasted_iota(jnp.int32, (8, 128), 1)
    row = lax.broadcasted_iota(jnp.int32, (8, 128), 0)
    block16 = lane // 16
    residue = lax.rem(lane, 16)

    def relative(device):
        return lax.rem(device // 4 - mx + 4, 4) * 4 + lax.rem(lax.rem(device, 4) - my_y + 4, 4)

    fetch_n.wait()
    fetch_v.wait()
    face = lax.broadcasted_iota(jnp.int32, (4, 8), 0)
    there = nbr_v[...]
    device = there // 8
    mirrored = face + 1 - 2 * lax.rem(face, 2)
    key = mirrored * 8 + lax.rem(there, 8)
    rank = jnp.zeros((4, 8), jnp.int32)
    least = jnp.zeros((8, 128), jnp.int32)
    most = jnp.zeros((8, 128), jnp.int32)
    for f in range(4):
        for s in range(8):
            n = nbr_s[f, s]
            other_key = (f ^ 1) * 8 + lax.rem(n, 8)
            before = (device == n // 8) & (key > other_key)
            rank = rank + jnp.where(before, 1, 0)
            most = jnp.where(lane == relative(n // 8), f * 8 + s, most)
            n = nbr_s[3 - f, 7 - s]
            least = jnp.where(lane == relative(n // 8), (3 - f) * 8 + 7 - s, least)
    place = jnp.where(
        device == me,
        jnp.minimum(mirrored, 2) * 8 + lax.rem(there, 8),
        OWN + (relative(device) - 1) * 2 + jnp.minimum(rank, 1),
    )
    tab_v[pl.ds(0, 8), :] = jnp.where(least >= 24, least - 8, least)
    tab_v[pl.ds(8, 8), :] = jnp.where(most >= 24, most - 8, most)
    tab_v[pl.ds(16, 4), pl.ds(0, 8)] = place
    to_scalar = pltpu.make_async_copy(tab_v, tab_s, local.at[3])
    to_scalar.start()

    for step in range(2):
        lrecv[step, pl.ds((ROWS - 4) * 8, 32), :] = jnp.zeros((32, 128), jnp.float32)

    def rows_of(c, s):
        return pl.multiple_of(c * 512 + s * CELLS, CELLS)

    def prepare(step, s, c, cells):
        high, low, sides = cells[7], cells[7], cells[0]
        for g in range(7):
            turned = pltpu.roll(cells[g], 16 * (g + 1), 1)
            high = jnp.where(block16 == g, turned, high)
            low = jnp.where(block16 == g + 1, turned, low)
        for g in range(1, 8):
            turned = pltpu.roll(cells[g], (30 * g) % 128, 1)
            sides = jnp.where(
                (residue == 16 - 2 * g) | (residue == 15 - 2 * g), turned, sides
            )
        mine[c, s] = low
        mine[c, 8 + s] = high
        mine[c, 16 + s] = sides
        faces[step][c][s] = low
        faces[step][c][8 + s] = high
        faces[step][c][16 + s] = sides
        lsend[step, pl.ds((NEAR + c) * 8 + s, 1), :] = cells[7][7:8]
        lsend[step, pl.ds((SLOT + NEAR + c) * 8 + s, 1), :] = cells[0][0:1]

    def functionals(step, now):
        side_by_side = jnp.concatenate([now[pl.ds(1024 + CELLS * s, CELLS), :] for s in range(8)], axis=1)
        got = product(cv[pl.ds(0, ROWS), pl.ds(0, CELLS)], side_by_side)
        for s in range(8):
            part = got[:, 128 * s : 128 * (s + 1)]
            lsend[step, pl.ds(s, NEAR, stride=8), :] = part[:NEAR]
            lsend[step, pl.ds(SLOT * 8 + s, NEAR, stride=8), :] = part[SLOT : SLOT + NEAR]
            lsend[step, pl.ds(2 * SLOT * 8 + s, 32, stride=8), :] = part[2 * SLOT :]

    def send_layer(step):
        copies = {}
        for o in FARTHER + [1, COUNT - 1]:
            first, count = MESSAGES[o]
            rows = pl.ds(first * 8, (SLOT if count == NEAR else count) * 8)
            copies[o] = pltpu.make_async_remote_copy(
                src_ref=lsend.at[step, rows, :],
                dst_ref=lrecv.at[step, rows, :],
                send_sem=ls.at[step, o],
                recv_sem=lr.at[step, o],
                device_id=layer_peer(o),
                device_id_type=MESH,
            )
            copies[o].start()
        return copies

    def send_strips(step, c):
        copies = []
        for dx, dy in PARTNERS:
            to = dx * 4 + dy
            back = (4 - dx) % 4 * 4 + (4 - dy) % 4
            ssend[step, c, 2 * to - 2] = mine[c, tab_s[0, to]]
            ssend[step, c, 2 * to - 1] = mine[c, tab_s[8, to]]
            copies.append(
                pltpu.make_async_remote_copy(
                    src_ref=ssend.at[step, c, pl.ds(2 * to - 2, 2)],
                    dst_ref=faces[step][c].at[pl.ds(OWN + 2 * back - 2, 2)],
                    send_sem=ps.at[step, c, to],
                    recv_sem=pr.at[step, c, back],
                    device_id=patch_peer(dx, dy),
                    device_id_type=MESH,
                )
            )
            copies[-1].start()
        return copies

    def tiles(ref, c, s):
        return [ref[pl.ds(rows_of(c, s) + 8 * g, 8), :] for g in range(8)]

    def local_part(step, now, later):
        def body(s, carry):
            level = refine[s]
            factor = jnp.where(level >= 1, 4.0, 1.0) * jnp.where(level >= 2, 4.0, 1.0)
            weight = grad_weight * factor
            cells = [now[pl.ds(rows_of(c, s), CELLS), :] for c in range(3)]
            lanes = lax.broadcasted_iota(jnp.int32, (CELLS, 128), 1)
            depth = lax.broadcasted_iota(jnp.int32, (CELLS, 128), 0)
            column = lax.rem(lanes, 16)
            square = cells[0] * cells[0] + cells[1] * cells[1] + cells[2] * cells[2]
            common = (
                1.0
                - 2.0 * grad_weight
                - 4.0 * weight
                - step_length * qv[pl.ds(pl.multiple_of(s * CELLS, CELLS), CELLS), :]
                - step_length * couple_weight * square
            )
            for c in range(3):
                x = cells[c]
                planar = (
                    jnp.where(lanes >= 16, pltpu.roll(x, 16, 1), 0.0)
                    + jnp.where(lanes < 112, pltpu.roll(x, 112, 1), 0.0)
                    + jnp.where(column > 0, pltpu.roll(x, 1, 1), 0.0)
                    + jnp.where(column < 15, pltpu.roll(x, 127, 1), 0.0)
                )
                vertical = jnp.where(depth > 0, pltpu.roll(x, 1, 0), 0.0) + jnp.where(
                    depth < CELLS - 1, pltpu.roll(x, CELLS - 1, 0), 0.0
                )
                new = (
                    x * (common - step_length * (1.0 - couple_weight) * x * x)
                    + weight * planar
                    + grad_weight * vertical
                )
                if c == 2:
                    new = new + step_length * field_values[step]
                later[pl.ds(rows_of(c, s), CELLS), :] = new
            return carry

        lax.fori_loop(0, 8, body, 0, unroll=2)
        side_by_side = jnp.concatenate([now[pl.ds(1024 + CELLS * s, CELLS), :] for s in range(8)], axis=1)
        field = product(cv[pl.ds(ROWS, CELLS), pl.ds(0, CELLS)], side_by_side)
        for s in range(8):
            dep[pl.ds(CELLS * s, CELLS), :] = field[:, 128 * s : 128 * (s + 1)]

    def add_field(step):
        heard = jnp.concatenate([lrecv[step, pl.ds(s, ROWS, stride=8), :] for s in range(8)], axis=1)
        field = product(cv[pl.ds(ROWS + CELLS, CELLS), pl.ds(0, ROWS)], heard)
        for s in range(8):
            rows = pl.ds(CELLS * s, CELLS)
            total = dep[rows, :] + field[:, 128 * s : 128 * (s + 1)]
            if step == 1:
                dep_out[rows, :] = total
            else:
                dep[rows, :] = total

    def finish(step, c, now, later, out_ref):
        def body(s, carry):
            level = refine[s]
            factor = jnp.where(level >= 1, 4.0, 1.0) * jnp.where(level >= 2, 4.0, 1.0)
            weight = grad_weight * factor
            south_w = jnp.where(lane < 16, weight, 0.0)
            north_w = jnp.where(lane >= 112, weight, 0.0)
            west_w = jnp.where(residue == 0, weight, 0.0)
            east_w = jnp.where(residue == 15, weight, 0.0)
            x = tiles(later, c, s)
            south = faces[step][c][tab_s[16, s]]
            north = faces[step][c][tab_s[17, s]]
            west = faces[step][c][tab_s[18, s]]
            east = faces[step][c][tab_s[19, s]]
            turned = [
                pltpu.roll(jnp.where(block16 == k, south, north), (128 - 16 * k) % 128, 1)
                for k in range(8)
            ]
            mixed = jnp.where(lax.rem(lane, 2) == 1, west, east)
            sides = [pltpu.roll(mixed, (-15 - 30 * k) % 128, 1) for k in range(-1, 8)]
            for g in range(8):
                x[g] = (
                    x[g]
                    + south_w * turned[g]
                    + north_w * turned[(g + 2) % 8]
                    + west_w * sides[g + 1]
                    + east_w * sides[g]
                )
            below = jnp.where(
                my == 0,
                now[pl.ds(rows_of(c, s), 1), :],
                lrecv[step, pl.ds((NEAR + c) * 8 + s, 1), :],
            )
            above = jnp.where(
                my == COUNT - 1,
                now[pl.ds(rows_of(c, s) + CELLS - 1, 1), :],
                lrecv[step, pl.ds((SLOT + NEAR + c) * 8 + s, 1), :],
            )
            x[0] = x[0] + jnp.where(row == 0, grad_weight * below, 0.0)
            x[7] = x[7] + jnp.where(row == 7, grad_weight * above, 0.0)
            if c == 2:
                whole = dep if step == 0 else dep_out
                field = tiles(whole, 0, s)
                x = [x[g] + step_length * field[g] for g in range(8)]
            for g in range(8):
                out_ref[pl.ds(rows_of(c, s) + 8 * g, 8), :] = x[g]
            if step == 0:
                prepare(1, s, c, x)
            return carry

        lax.fori_loop(0, 8, body, 0, unroll=8)

    def wait_recv(copies):
        for copy in copies:
            copy.wait_recv()

    def near(copies):
        return [copies[o] for o in (1, COUNT - 1)]

    def far(copies):
        return [copies[o] for o in FARTHER]

    fetch_p.wait()
    fetch_c.wait()
    functionals(0, cur)

    def first(s, carry):
        for c in range(3):
            prepare(0, s, c, tiles(cur, c, s))
        return carry

    lax.fori_loop(0, 8, first, 0)
    to_scalar.wait()
    pl.semaphore_wait(barrier, 2 * (COUNT - 1))
    layer0 = send_layer(0)
    strips0 = [send_strips(0, c) for c in range(3)]
    fetch_q.wait()
    fetch_l.wait()
    local_part(0, cur, nxt)
    wait_recv(near(layer0))
    strips1 = []
    for c in range(3):
        wait_recv(strips0[c])
        if c == 2:
            wait_recv(far(layer0))
            add_field(0)
        finish(0, c, cur, nxt, nxt)
        if c == 2:
            functionals(1, nxt)
            layer1 = send_layer(1)
        strips1.append(send_strips(1, c))
    local_part(1, nxt, cur)
    wait_recv(near(layer1))
    for c in range(3):
        wait_recv(strips1[c])
        if c == 2:
            wait_recv(far(layer1))
            add_field(1)
        finish(1, c, nxt, cur, out)
    for copy in [*layer0.values(), *layer1.values(), *sum(strips0 + strips1, [])]:
        copy.wait_send()


def deliver(final, field, final_out, field_out, done):
    copies = [
        pltpu.make_async_copy(final, final_out, done.at[0]),
        pltpu.make_async_copy(field, field_out, done.at[1]),
    ]
    for copy in copies:
        copy.start()
    for copy in copies:
        copy.wait()


def on_device(polarization, quadratic, neighbours, refinement):
    vmem = pl.BlockSpec(memory_space=pltpu.VMEM)
    hbm = pl.BlockSpec(memory_space=pltpu.HBM)
    dma = pltpu.SemaphoreType.DMA
    f32 = jnp.float32
    final, field = pl.pallas_call(
        kernel,
        out_shape=(
            pltpu.VMEM((1536, 128), f32),
            pltpu.VMEM((512, 128), f32),
        ),
        in_specs=[hbm] * 5,
        out_specs=(vmem, vmem),
        scratch_shapes=[
            pltpu.SMEM((4, 8), jnp.int32),
            pltpu.VMEM((4, 8), jnp.int32),
            pltpu.SMEM((8,), jnp.int32),
            pltpu.VMEM((1536, 128), f32),
            pltpu.VMEM((1536, 128), f32),
            pltpu.VMEM((512, 128), f32),
            pltpu.VMEM((3 * CELLS, 128), f32),
            pltpu.VMEM((512, 128), f32),
            pltpu.VMEM((3, OWN, 8, 128), f32),
            *[pltpu.VMEM((OWN + 30, 8, 128), f32)] * 6,
            pltpu.VMEM((2, 3, 30, 8, 128), f32),
            pltpu.VMEM((2, ROWS * 8, 128), f32),
            pltpu.VMEM((2, ROWS * 8, 128), f32),
            pltpu.VMEM((24, 128), jnp.int32),
            pltpu.SMEM((24, 128), jnp.int32),
            dma((2, 3, 16)),
            dma((2, 3, 16)),
            dma((2, 16)),
            dma((2, 16)),
            dma((7,)),
        ],
        compiler_params=pltpu.CompilerParams(
            collective_id=0, has_side_effects=True, vmem_limit_bytes=32 << 20
        ),
    )(
        *(
            pltpu.with_memory_space_constraint(x, pltpu.HBM)
            for x in (
                polarization.reshape(1536, 128),
                quadratic.reshape(512, 128),
                neighbours,
                refinement,
                jnp.asarray(layer_constants()),
            )
        )
    )
    final, field = pl.pallas_call(
        deliver,
        out_shape=(
            jax.ShapeDtypeStruct((1536, 128), f32),
            jax.ShapeDtypeStruct((512, 128), f32),
        ),
        in_specs=[vmem, vmem],
        out_specs=(hbm, hbm),
        scratch_shapes=[dma((2,))],
    )(*(pltpu.with_memory_space_constraint(x, pltpu.VMEM) for x in (final, field)))
    return final.reshape(polarization.shape), field.reshape(quadratic.shape)


def solution(mesh):
    in_specs = (
        P(None, "patch", "layer", None),
        P("patch", "layer", None),
        P(None, "patch"),
        P("patch"),
    )
    out_specs = (P(None, "patch", "layer", None), P("patch", "layer", None))
    return jax.shard_map(
        on_device, mesh=mesh, in_specs=in_specs, out_specs=out_specs, check_vma=False
    )
```

```python
import functools
import math

import jax
import jax.numpy as jnp
import numpy as np
from jax import lax
from jax.experimental import pallas as pl
from jax.experimental.pallas import tpu as pltpu
from jax.sharding import PartitionSpec as P

step_length = 0.1
grad_weight = 0.01
couple_weight = 0.5
screening = 0.0001
damping = 2.0 / 3.0
field_values = (0.8 * math.sin(0.6 * math.pi), 0.8 * math.sin(0.8 * math.pi))

MESH = pl.DeviceIdType.MESH
HIGHEST = lax.Precision.HIGHEST

CELLS = 64
COUNT = 16
NEAR = 13
SLOT = 16
SENT = 60
ROWS = 64
OWN = 24

PARTNERS = sorted(
    [(dx, dy) for dx in range(4) for dy in range(4) if dx or dy],
    key=lambda d: -(min(d[0], 4 - d[0]) + min(d[1], 4 - d[1])),
)
MESSAGES = {1: (0, NEAR), COUNT - 1: (SLOT, NEAR), 2: (2 * SLOT, 3), COUNT - 2: (2 * SLOT + 3, 3)}
MESSAGES.update({o: (2 * SLOT + 2 * o, 2) for o in range(3, COUNT - 2)})
FARTHER = sorted(range(2, COUNT - 1), key=lambda o: -min(o, COUNT - o))


def column_cycle(source, level):
    diagonal = 2.0 * 0.25**level + screening
    if source.shape[0] == 1:
        return source / diagonal

    def apply(v):
        padded = np.pad(v, ((1, 1), (0, 0)))
        return (2.0 * v - padded[:-2] - padded[2:]) * 0.25**level + screening * v

    correction = damping * source / diagonal
    residual = source - apply(correction)
    coarse = (residual[0::2] + residual[1::2]) * 0.5
    correction = correction + np.repeat(column_cycle(coarse, level + 1), 2, axis=0)
    return correction + damping * (source - apply(correction)) / diagonal


def field_operator(cells):
    padded = np.pad(np.eye(cells), ((1, 1), (0, 0)), mode="edge")
    charge = -(padded[2:] - padded[:-2]) * 0.5
    rimmed = np.pad(column_cycle(charge, 0), ((1, 1), (0, 0)))
    return -(rimmed[2:] - rimmed[:-2]) * 0.5


def row_basis(block, rank):
    rest = block.copy()
    rows = np.zeros((rank, block.shape[1]))
    for k in range(rank):
        norms = np.sum(rest * rest, axis=1)
        best = int(np.argmax(norms))
        if norms[best] < 1e-24:
            break
        row = rest[best]
        for _ in range(2):
            for earlier in rows[:k]:
                row = row - np.sum(row * earlier) * earlier
        row = row / np.sqrt(np.sum(row * row))
        rows[k] = row
        rest = rest - np.sum(rest * row, axis=1, keepdims=True) * row
    return rows


def project(block, rows):
    return np.stack([np.sum(block * row, axis=1) for row in rows], axis=1)


@functools.cache
def layer_constants():
    whole = field_operator(CELLS * COUNT)

    def block(d, e):
        return whole[d * CELLS : (d + 1) * CELLS, e * CELLS : (e + 1) * CELLS]

    table = np.zeros((COUNT, 3 * CELLS, 128))
    for e in range(COUNT):
        table[e, ROWS : ROWS + CELLS, :CELLS] = block(e, e)
        for o, (first, rank) in MESSAGES.items():
            d = (e + o) % COUNT
            basis = row_basis(block(d, e), rank)
            table[e, first : first + rank, :CELLS] = basis
            table[d, ROWS + CELLS :, first : first + rank] = project(block(d, e), basis)
    return table.astype(np.float32)


def product(left, right):
    return jnp.dot(left, right, precision=HIGHEST, preferred_element_type=jnp.float32)


def kernel(
    pol, quad, nbr, levels, consts,
    out, dep_out,
    nbr_s, nbr_v, refine, cur, nxt, qv, cv, dep, mine,
    faces00, faces01, faces02, faces10, faces11, faces12,
    ssend, lsend, lrecv, tab_v, tab_s, ps, pr, ls, lr, local,
):
    faces = ((faces00, faces01, faces02), (faces10, faces11, faces12))
    me = lax.axis_index("patch")
    my = lax.axis_index("layer")
    mx, my_y = me // 4, lax.rem(me, 4)

    def patch_peer(dx, dy):
        return (lax.rem(mx + dx, 4) * 4 + lax.rem(my_y + dy, 4), my)

    def layer_peer(o):
        return (me, lax.rem(my + o, COUNT))

    barrier = pltpu.get_barrier_semaphore()
    for dx, dy in PARTNERS:
        pl.semaphore_signal(barrier, inc=1, device_id=patch_peer(dx, dy), device_id_type=MESH)
    for o in range(1, COUNT):
        pl.semaphore_signal(barrier, inc=1, device_id=layer_peer(o), device_id_type=MESH)

    fetch_p = pltpu.make_async_copy(pol, cur, local.at[0])
    fetch_c = pltpu.make_async_copy(consts.at[my], cv, local.at[1])
    fetch_q = pltpu.make_async_copy(quad, qv, local.at[2])
    fetch_n = pltpu.make_async_copy(nbr, nbr_s, local.at[4])
    fetch_v = pltpu.make_async_copy(nbr, nbr_v, local.at[5])
    fetch_l = pltpu.make_async_copy(levels, refine, local.at[6])
    fetch_n.start()
    fetch_v.start()
    fetch_p.start()
    fetch_c.start()
    fetch_l.start()
    fetch_q.start()

    lane = lax.broadcasted_iota(jnp.int32, (8, 128), 1)
    row = lax.broadcasted_iota(jnp.int32, (8, 128), 0)
    block16 = lane // 16
    residue = lax.rem(lane, 16)

    def relative(device):
        return lax.rem(device // 4 - mx + 4, 4) * 4 + lax.rem(lax.rem(device, 4) - my_y + 4, 4)

    fetch_n.wait()
    fetch_v.wait()
    face = lax.broadcasted_iota(jnp.int32, (4, 8), 0)
    there = nbr_v[...]
    device = there // 8
    mirrored = face + 1 - 2 * lax.rem(face, 2)
    key = mirrored * 8 + lax.rem(there, 8)
    rank = jnp.zeros((4, 8), jnp.int32)
    least = jnp.zeros((8, 128), jnp.int32)
    most = jnp.zeros((8, 128), jnp.int32)
    for f in range(4):
        for s in range(8):
            n = nbr_s[f, s]
            other_key = (f ^ 1) * 8 + lax.rem(n, 8)
            before = (device == n // 8) & (key > other_key)
            rank = rank + jnp.where(before, 1, 0)
            most = jnp.where(lane == relative(n // 8), f * 8 + s, most)
            n = nbr_s[3 - f, 7 - s]
            least = jnp.where(lane == relative(n // 8), (3 - f) * 8 + 7 - s, least)
    place = jnp.where(
        device == me,
        jnp.minimum(mirrored, 2) * 8 + lax.rem(there, 8),
        OWN + (relative(device) - 1) * 2 + jnp.minimum(rank, 1),
    )
    tab_v[pl.ds(0, 8), :] = jnp.where(least >= 24, least - 8, least)
    tab_v[pl.ds(8, 8), :] = jnp.where(most >= 24, most - 8, most)
    tab_v[pl.ds(16, 4), pl.ds(0, 8)] = place
    to_scalar = pltpu.make_async_copy(tab_v, tab_s, local.at[3])
    to_scalar.start()

    for step in range(2):
        lrecv[step, pl.ds((ROWS - 4) * 8, 32), :] = jnp.zeros((32, 128), jnp.float32)

    def rows_of(c, s):
        return pl.multiple_of(c * 512 + s * CELLS, CELLS)

    def prepare(step, s, c, cells):
        high, low, sides = cells[7], cells[7], cells[0]
        for g in range(7):
            turned = pltpu.roll(cells[g], 16 * (g + 1), 1)
            high = jnp.where(block16 == g, turned, high)
            low = jnp.where(block16 == g + 1, turned, low)
        for g in range(1, 8):
            turned = pltpu.roll(cells[g], (30 * g) % 128, 1)
            sides = jnp.where(
                (residue == 16 - 2 * g) | (residue == 15 - 2 * g), turned, sides
            )
        mine[c, s] = low
        mine[c, 8 + s] = high
        mine[c, 16 + s] = sides
        faces[step][c][s] = low
        faces[step][c][8 + s] = high
        faces[step][c][16 + s] = sides
        lsend[step, pl.ds((NEAR + c) * 8 + s, 1), :] = cells[7][7:8]
        lsend[step, pl.ds((SLOT + NEAR + c) * 8 + s, 1), :] = cells[0][0:1]

    def functionals(step, now):
        side_by_side = jnp.concatenate([now[pl.ds(1024 + CELLS * s, CELLS), :] for s in range(8)], axis=1)
        got = product(cv[pl.ds(0, ROWS), pl.ds(0, CELLS)], side_by_side)
        for s in range(8):
            part = got[:, 128 * s : 128 * (s + 1)]
            lsend[step, pl.ds(s, NEAR, stride=8), :] = part[:NEAR]
            lsend[step, pl.ds(SLOT * 8 + s, NEAR, stride=8), :] = part[SLOT : SLOT + NEAR]
            lsend[step, pl.ds(2 * SLOT * 8 + s, 32, stride=8), :] = part[2 * SLOT :]

    def send_layer(step):
        for o in FARTHER + [1, COUNT - 1]:
            first, count = MESSAGES[o]
            rows = pl.ds(first * 8, (SLOT if count == NEAR else count) * 8)
            pltpu.make_async_remote_copy(
                src_ref=lsend.at[step, rows, :],
                dst_ref=lrecv.at[step, rows, :],
                send_sem=ls.at[step],
                recv_sem=lr.at[step, 0 if count == NEAR else 1],
                device_id=layer_peer(o),
                device_id_type=MESH,
            ).start()

    def send_strips(step, c):
        for dx, dy in PARTNERS:
            to = dx * 4 + dy
            back = (4 - dx) % 4 * 4 + (4 - dy) % 4
            ssend[step, c, 2 * to - 2] = mine[c, tab_s[0, to]]
            ssend[step, c, 2 * to - 1] = mine[c, tab_s[8, to]]
            pltpu.make_async_remote_copy(
                src_ref=ssend.at[step, c, pl.ds(2 * to - 2, 2)],
                dst_ref=faces[step][c].at[pl.ds(OWN + 2 * back - 2, 2)],
                send_sem=ps.at[0],
                recv_sem=pr.at[step, c],
                device_id=patch_peer(dx, dy),
                device_id_type=MESH,
            ).start()

    def tiles(ref, c, s):
        return [ref[pl.ds(rows_of(c, s) + 8 * g, 8), :] for g in range(8)]

    def local_part(step, now, later):
        def body(s, carry):
            level = refine[s]
            factor = jnp.where(level >= 1, 4.0, 1.0) * jnp.where(level >= 2, 4.0, 1.0)
            weight = grad_weight * factor
            cells = [now[pl.ds(rows_of(c, s), CELLS), :] for c in range(3)]
            lanes = lax.broadcasted_iota(jnp.int32, (CELLS, 128), 1)
            depth = lax.broadcasted_iota(jnp.int32, (CELLS, 128), 0)
            column = lax.rem(lanes, 16)
            square = cells[0] * cells[0] + cells[1] * cells[1] + cells[2] * cells[2]
            common = (
                1.0
                - 2.0 * grad_weight
                - 4.0 * weight
                - step_length * qv[pl.ds(pl.multiple_of(s * CELLS, CELLS), CELLS), :]
                - step_length * couple_weight * square
            )
            for c in range(3):
                x = cells[c]
                planar = (
                    jnp.where(lanes >= 16, pltpu.roll(x, 16, 1), 0.0)
                    + jnp.where(lanes < 112, pltpu.roll(x, 112, 1), 0.0)
                    + jnp.where(column > 0, pltpu.roll(x, 1, 1), 0.0)
                    + jnp.where(column < 15, pltpu.roll(x, 127, 1), 0.0)
                )
                vertical = jnp.where(depth > 0, pltpu.roll(x, 1, 0), 0.0) + jnp.where(
                    depth < CELLS - 1, pltpu.roll(x, CELLS - 1, 0), 0.0
                )
                new = (
                    x * (common - step_length * (1.0 - couple_weight) * x * x)
                    + weight * planar
                    + grad_weight * vertical
                )
                if c == 2:
                    new = new + step_length * field_values[step]
                later[pl.ds(rows_of(c, s), CELLS), :] = new
            return carry

        lax.fori_loop(0, 8, body, 0, unroll=2)
        side_by_side = jnp.concatenate([now[pl.ds(1024 + CELLS * s, CELLS), :] for s in range(8)], axis=1)
        field = product(cv[pl.ds(ROWS, CELLS), pl.ds(0, CELLS)], side_by_side)
        for s in range(8):
            dep[pl.ds(CELLS * s, CELLS), :] = field[:, 128 * s : 128 * (s + 1)]

    def add_field(step):
        heard = jnp.concatenate([lrecv[step, pl.ds(s, ROWS, stride=8), :] for s in range(8)], axis=1)
        field = product(cv[pl.ds(ROWS + CELLS, CELLS), pl.ds(0, ROWS)], heard)
        for s in range(8):
            rows = pl.ds(CELLS * s, CELLS)
            total = dep[rows, :] + field[:, 128 * s : 128 * (s + 1)]
            if step == 1:
                dep_out[rows, :] = total
            else:
                dep[rows, :] = total

    def finish(step, c, now, later, out_ref):
        def body(s, carry):
            level = refine[s]
            factor = jnp.where(level >= 1, 4.0, 1.0) * jnp.where(level >= 2, 4.0, 1.0)
            weight = grad_weight * factor
            south_w = jnp.where(lane < 16, weight, 0.0)
            north_w = jnp.where(lane >= 112, weight, 0.0)
            west_w = jnp.where(residue == 0, weight, 0.0)
            east_w = jnp.where(residue == 15, weight, 0.0)
            x = tiles(later, c, s)
            south = faces[step][c][tab_s[16, s]]
            north = faces[step][c][tab_s[17, s]]
            west = faces[step][c][tab_s[18, s]]
            east = faces[step][c][tab_s[19, s]]
            turned = [
                pltpu.roll(jnp.where(block16 == k, south, north), (128 - 16 * k) % 128, 1)
                for k in range(8)
            ]
            mixed = jnp.where(lax.rem(lane, 2) == 1, west, east)
            sides = [pltpu.roll(mixed, (-15 - 30 * k) % 128, 1) for k in range(-1, 8)]
            for g in range(8):
                x[g] = (
                    x[g]
                    + south_w * turned[g]
                    + north_w * turned[(g + 2) % 8]
                    + west_w * sides[g + 1]
                    + east_w * sides[g]
                )
            below = jnp.where(
                my == 0,
                now[pl.ds(rows_of(c, s), 1), :],
                lrecv[step, pl.ds((NEAR + c) * 8 + s, 1), :],
            )
            above = jnp.where(
                my == COUNT - 1,
                now[pl.ds(rows_of(c, s) + CELLS - 1, 1), :],
                lrecv[step, pl.ds((SLOT + NEAR + c) * 8 + s, 1), :],
            )
            x[0] = x[0] + jnp.where(row == 0, grad_weight * below, 0.0)
            x[7] = x[7] + jnp.where(row == 7, grad_weight * above, 0.0)
            if c == 2:
                whole = dep if step == 0 else dep_out
                field = tiles(whole, 0, s)
                x = [x[g] + step_length * field[g] for g in range(8)]
            for g in range(8):
                out_ref[pl.ds(rows_of(c, s) + 8 * g, 8), :] = x[g]
            if step == 0:
                prepare(1, s, c, x)
            return carry

        lax.fori_loop(0, 8, body, 0, unroll=8)

    def wait_bytes(ref, sem):
        pltpu.make_async_copy(ref, ref, sem).wait()

    def wait_near(step):
        wait_bytes(lrecv.at[step, pl.ds(0, 2 * SLOT * 8), :], lr.at[step, 0])

    def wait_far(step):
        wait_bytes(lrecv.at[step, pl.ds(2 * SLOT * 8, (SENT - 2 * SLOT) * 8), :], lr.at[step, 1])

    def wait_strips(step, c):
        wait_bytes(faces[step][c].at[pl.ds(OWN, 30)], pr.at[step, c])

    fetch_p.wait()
    fetch_c.wait()
    functionals(0, cur)

    def first(s, carry):
        for c in range(3):
            prepare(0, s, c, tiles(cur, c, s))
        return carry

    lax.fori_loop(0, 8, first, 0)
    to_scalar.wait()
    pl.semaphore_wait(barrier, 2 * (COUNT - 1))
    send_layer(0)
    for c in range(3):
        send_strips(0, c)
    fetch_q.wait()
    fetch_l.wait()
    local_part(0, cur, nxt)
    wait_near(0)
    for c in range(3):
        wait_strips(0, c)
        if c == 2:
            wait_far(0)
            add_field(0)
        finish(0, c, cur, nxt, nxt)
        if c == 2:
            functionals(1, nxt)
            send_layer(1)
        send_strips(1, c)
    local_part(1, nxt, cur)
    wait_near(1)
    for c in range(3):
        wait_strips(1, c)
        if c == 2:
            wait_far(1)
            add_field(1)
        finish(1, c, nxt, cur, out)
    for step in range(2):
        wait_bytes(lsend.at[step, pl.ds(0, SENT * 8), :], ls.at[step])
    wait_bytes(ssend, ps.at[0])


def deliver(final, field, final_out, field_out, done):
    copies = [
        pltpu.make_async_copy(final, final_out, done.at[0]),
        pltpu.make_async_copy(field, field_out, done.at[1]),
    ]
    for copy in copies:
        copy.start()
    for copy in copies:
        copy.wait()


def on_device(polarization, quadratic, neighbours, refinement):
    vmem = pl.BlockSpec(memory_space=pltpu.VMEM)
    hbm = pl.BlockSpec(memory_space=pltpu.HBM)
    dma = pltpu.SemaphoreType.DMA
    f32 = jnp.float32
    final, field = pl.pallas_call(
        kernel,
        out_shape=(
            pltpu.VMEM((1536, 128), f32),
            pltpu.VMEM((512, 128), f32),
        ),
        in_specs=[hbm] * 5,
        out_specs=(vmem, vmem),
        scratch_shapes=[
            pltpu.SMEM((4, 8), jnp.int32),
            pltpu.VMEM((4, 8), jnp.int32),
            pltpu.SMEM((8,), jnp.int32),
            pltpu.VMEM((1536, 128), f32),
            pltpu.VMEM((1536, 128), f32),
            pltpu.VMEM((512, 128), f32),
            pltpu.VMEM((3 * CELLS, 128), f32),
            pltpu.VMEM((512, 128), f32),
            pltpu.VMEM((3, OWN, 8, 128), f32),
            *[pltpu.VMEM((OWN + 30, 8, 128), f32)] * 6,
            pltpu.VMEM((2, 3, 30, 8, 128), f32),
            pltpu.VMEM((2, ROWS * 8, 128), f32),
            pltpu.VMEM((2, ROWS * 8, 128), f32),
            pltpu.VMEM((24, 128), jnp.int32),
            pltpu.SMEM((24, 128), jnp.int32),
            dma((1,)),
            dma((2, 3)),
            dma((2,)),
            dma((2, 2)),
            dma((7,)),
        ],
        compiler_params=pltpu.CompilerParams(
            collective_id=0, has_side_effects=True, vmem_limit_bytes=32 << 20
        ),
    )(
        *(
            pltpu.with_memory_space_constraint(x, pltpu.HBM)
            for x in (
                polarization.reshape(1536, 128),
                quadratic.reshape(512, 128),
                neighbours,
                refinement,
                jnp.asarray(layer_constants()),
            )
        )
    )
    final, field = pl.pallas_call(
        deliver,
        out_shape=(
            jax.ShapeDtypeStruct((1536, 128), f32),
            jax.ShapeDtypeStruct((512, 128), f32),
        ),
        in_specs=[vmem, vmem],
        out_specs=(hbm, hbm),
        scratch_shapes=[dma((2,))],
    )(*(pltpu.with_memory_space_constraint(x, pltpu.VMEM) for x in (final, field)))
    return final.reshape(polarization.shape), field.reshape(quadratic.shape)


def solution(mesh):
    in_specs = (
        P(None, "patch", "layer", None),
        P("patch", "layer", None),
        P(None, "patch"),
        P("patch"),
    )
    out_specs = (P(None, "patch", "layer", None), P("patch", "layer", None))
    return jax.shard_map(
        on_device, mesh=mesh, in_specs=in_specs, out_specs=out_specs, check_vma=False
    )
```

```python
import functools
import math

import jax
import jax.numpy as jnp
import numpy as np
from jax import lax
from jax.experimental import pallas as pl
from jax.experimental.pallas import tpu as pltpu
from jax.sharding import PartitionSpec as P

step_length = 0.1
grad_weight = 0.01
couple_weight = 0.5
screening = 0.0001
damping = 2.0 / 3.0
field_values = (0.8 * math.sin(0.6 * math.pi), 0.8 * math.sin(0.8 * math.pi))

MESH = pl.DeviceIdType.MESH
HIGHEST = lax.Precision.HIGHEST

CELLS = 64
COUNT = 16
NEAR = 13
SLOT = 16
SENT = 60
ROWS = 64
OWN = 24

PARTNERS = sorted(
    [(dx, dy) for dx in range(4) for dy in range(4) if dx or dy],
    key=lambda d: -(min(d[0], 4 - d[0]) + min(d[1], 4 - d[1])),
)
MESSAGES = {1: (0, NEAR), COUNT - 1: (SLOT, NEAR), 2: (2 * SLOT, 3), COUNT - 2: (2 * SLOT + 3, 3)}
MESSAGES.update({o: (2 * SLOT + 2 * o, 2) for o in range(3, COUNT - 2)})
FARTHER = sorted(range(2, COUNT - 1), key=lambda o: -min(o, COUNT - o))


def column_cycle(source, level):
    diagonal = 2.0 * 0.25**level + screening
    if source.shape[0] == 1:
        return source / diagonal

    def apply(v):
        padded = np.pad(v, ((1, 1), (0, 0)))
        return (2.0 * v - padded[:-2] - padded[2:]) * 0.25**level + screening * v

    correction = damping * source / diagonal
    residual = source - apply(correction)
    coarse = (residual[0::2] + residual[1::2]) * 0.5
    correction = correction + np.repeat(column_cycle(coarse, level + 1), 2, axis=0)
    return correction + damping * (source - apply(correction)) / diagonal


def field_operator(cells):
    padded = np.pad(np.eye(cells), ((1, 1), (0, 0)), mode="edge")
    charge = -(padded[2:] - padded[:-2]) * 0.5
    rimmed = np.pad(column_cycle(charge, 0), ((1, 1), (0, 0)))
    return -(rimmed[2:] - rimmed[:-2]) * 0.5


def row_basis(block, rank):
    rest = block.copy()
    rows = np.zeros((rank, block.shape[1]))
    for k in range(rank):
        norms = np.sum(rest * rest, axis=1)
        best = int(np.argmax(norms))
        if norms[best] < 1e-24:
            break
        row = rest[best]
        for _ in range(2):
            for earlier in rows[:k]:
                row = row - np.sum(row * earlier) * earlier
        row = row / np.sqrt(np.sum(row * row))
        rows[k] = row
        rest = rest - np.sum(rest * row, axis=1, keepdims=True) * row
    return rows


def project(block, rows):
    return np.stack([np.sum(block * row, axis=1) for row in rows], axis=1)


@functools.cache
def layer_constants():
    whole = field_operator(CELLS * COUNT)

    def block(d, e):
        return whole[d * CELLS : (d + 1) * CELLS, e * CELLS : (e + 1) * CELLS]

    table = np.zeros((COUNT, 3 * CELLS, 128))
    for e in range(COUNT):
        table[e, ROWS : ROWS + CELLS, :CELLS] = block(e, e)
        for o, (first, rank) in MESSAGES.items():
            d = (e + o) % COUNT
            basis = row_basis(block(d, e), rank)
            table[e, first : first + rank, :CELLS] = basis
            table[d, ROWS + CELLS :, first : first + rank] = project(block(d, e), basis)
    return table.astype(np.float32)


def product(left, right):
    return jnp.dot(left, right, precision=HIGHEST, preferred_element_type=jnp.float32)


def kernel(
    pol, quad, nbr, levels, consts,
    out, dep_out,
    nbr_s, nbr_v, refine, cur, nxt, qv, cv, dep, mine,
    faces00, faces01, faces02, faces10, faces11, faces12,
    ssend, lsend, lrecv, tab_v, tab_s, ps, pr, ls, lr, local,
):
    faces = ((faces00, faces01, faces02), (faces10, faces11, faces12))
    me = lax.axis_index("patch")
    my = lax.axis_index("layer")
    mx, my_y = me // 4, lax.rem(me, 4)

    def patch_peer(dx, dy):
        return (lax.rem(mx + dx, 4) * 4 + lax.rem(my_y + dy, 4), my)

    def layer_peer(o):
        return (me, lax.rem(my + o, COUNT))

    barrier = pltpu.get_barrier_semaphore()
    for dx, dy in PARTNERS:
        pl.semaphore_signal(barrier, inc=1, device_id=patch_peer(dx, dy), device_id_type=MESH)
    for o in range(1, COUNT):
        pl.semaphore_signal(barrier, inc=1, device_id=layer_peer(o), device_id_type=MESH)

    fetch_p = pltpu.make_async_copy(pol, cur, local.at[0])
    fetch_c = pltpu.make_async_copy(consts.at[my], cv, local.at[1])
    fetch_q = pltpu.make_async_copy(quad, qv, local.at[2])
    fetch_n = pltpu.make_async_copy(nbr, nbr_s, local.at[4])
    fetch_v = pltpu.make_async_copy(nbr, nbr_v, local.at[5])
    fetch_l = pltpu.make_async_copy(levels, refine, local.at[6])
    fetch_n.start()
    fetch_v.start()
    fetch_p.start()
    fetch_c.start()
    fetch_l.start()
    fetch_q.start()

    lane = lax.broadcasted_iota(jnp.int32, (8, 128), 1)
    row = lax.broadcasted_iota(jnp.int32, (8, 128), 0)
    block16 = lane // 16
    residue = lax.rem(lane, 16)

    def relative(device):
        return lax.rem(device // 4 - mx + 4, 4) * 4 + lax.rem(lax.rem(device, 4) - my_y + 4, 4)

    fetch_n.wait()
    fetch_v.wait()
    face = lax.broadcasted_iota(jnp.int32, (4, 8), 0)
    there = nbr_v[...]
    device = there // 8
    mirrored = face + 1 - 2 * lax.rem(face, 2)
    key = mirrored * 8 + lax.rem(there, 8)
    rank = jnp.zeros((4, 8), jnp.int32)
    least = jnp.zeros((8, 128), jnp.int32)
    most = jnp.zeros((8, 128), jnp.int32)
    for f in range(4):
        for s in range(8):
            n = nbr_s[f, s]
            other_key = (f ^ 1) * 8 + lax.rem(n, 8)
            before = (device == n // 8) & (key > other_key)
            rank = rank + jnp.where(before, 1, 0)
            most = jnp.where(lane == relative(n // 8), f * 8 + s, most)
            n = nbr_s[3 - f, 7 - s]
            least = jnp.where(lane == relative(n // 8), (3 - f) * 8 + 7 - s, least)
    place = jnp.where(
        device == me,
        jnp.minimum(mirrored, 2) * 8 + lax.rem(there, 8),
        OWN + (relative(device) - 1) * 2 + jnp.minimum(rank, 1),
    )
    tab_v[pl.ds(0, 8), :] = jnp.where(least >= 24, least - 8, least)
    tab_v[pl.ds(8, 8), :] = jnp.where(most >= 24, most - 8, most)
    tab_v[pl.ds(16, 4), pl.ds(0, 8)] = place
    to_scalar = pltpu.make_async_copy(tab_v, tab_s, local.at[3])
    to_scalar.start()

    for step in range(2):
        lrecv[step, pl.ds((ROWS - 4) * 8, 32), :] = jnp.zeros((32, 128), jnp.float32)

    def rows_of(c, s):
        return pl.multiple_of(c * 512 + s * CELLS, CELLS)

    def prepare(step, s, c, cells):
        high, low, sides = cells[7], cells[7], cells[0]
        for g in range(7):
            turned = pltpu.roll(cells[g], 16 * (g + 1), 1)
            high = jnp.where(block16 == g, turned, high)
            low = jnp.where(block16 == g + 1, turned, low)
        for g in range(1, 8):
            turned = pltpu.roll(cells[g], (30 * g) % 128, 1)
            sides = jnp.where(
                (residue == 16 - 2 * g) | (residue == 15 - 2 * g), turned, sides
            )
        mine[c, s] = low
        mine[c, 8 + s] = high
        mine[c, 16 + s] = sides
        faces[step][c][s] = low
        faces[step][c][8 + s] = high
        faces[step][c][16 + s] = sides
        lsend[step, pl.ds((NEAR + c) * 8 + s, 1), :] = cells[7][7:8]
        lsend[step, pl.ds((SLOT + NEAR + c) * 8 + s, 1), :] = cells[0][0:1]

    def functionals(step, now):
        side_by_side = jnp.concatenate([now[pl.ds(1024 + CELLS * s, CELLS), :] for s in range(8)], axis=1)
        got = product(cv[pl.ds(0, ROWS), pl.ds(0, CELLS)], side_by_side)
        for s in range(8):
            part = got[:, 128 * s : 128 * (s + 1)]
            lsend[step, pl.ds(s, NEAR, stride=8), :] = part[:NEAR]
            lsend[step, pl.ds(SLOT * 8 + s, NEAR, stride=8), :] = part[SLOT : SLOT + NEAR]
            lsend[step, pl.ds(2 * SLOT * 8 + s, 32, stride=8), :] = part[2 * SLOT :]

    def send_layer(step):
        pieces = []
        for part in range(4):
            for o in (1, COUNT - 1):
                pieces.append((o, MESSAGES[o][0] + part * SLOT // 4, SLOT // 4))
        pieces += [(o, *MESSAGES[o]) for o in FARTHER]
        for o, first, count in pieces:
            rows = pl.ds(first * 8, count * 8)
            pltpu.make_async_remote_copy(
                src_ref=lsend.at[step, rows, :],
                dst_ref=lrecv.at[step, rows, :],
                send_sem=ls.at[step],
                recv_sem=lr.at[step, 0 if o in (1, COUNT - 1) else 1],
                device_id=layer_peer(o),
                device_id_type=MESH,
            ).start()

    def send_strips(step, c):
        for dx, dy in PARTNERS:
            to = dx * 4 + dy
            back = (4 - dx) % 4 * 4 + (4 - dy) % 4
            ssend[step, c, 2 * to - 2] = mine[c, tab_s[0, to]]
            ssend[step, c, 2 * to - 1] = mine[c, tab_s[8, to]]
            pltpu.make_async_remote_copy(
                src_ref=ssend.at[step, c, pl.ds(2 * to - 2, 2)],
                dst_ref=faces[step][c].at[pl.ds(OWN + 2 * back - 2, 2)],
                send_sem=ps.at[0],
                recv_sem=pr.at[step, c],
                device_id=patch_peer(dx, dy),
                device_id_type=MESH,
            ).start()

    def tiles(ref, c, s):
        return [ref[pl.ds(rows_of(c, s) + 8 * g, 8), :] for g in range(8)]

    def local_part(step, now, later):
        def body(s, carry):
            level = refine[s]
            factor = jnp.where(level >= 1, 4.0, 1.0) * jnp.where(level >= 2, 4.0, 1.0)
            weight = grad_weight * factor
            cells = [now[pl.ds(rows_of(c, s), CELLS), :] for c in range(3)]
            lanes = lax.broadcasted_iota(jnp.int32, (CELLS, 128), 1)
            depth = lax.broadcasted_iota(jnp.int32, (CELLS, 128), 0)
            column = lax.rem(lanes, 16)
            square = cells[0] * cells[0] + cells[1] * cells[1] + cells[2] * cells[2]
            common = (
                1.0
                - 2.0 * grad_weight
                - 4.0 * weight
                - step_length * qv[pl.ds(pl.multiple_of(s * CELLS, CELLS), CELLS), :]
                - step_length * couple_weight * square
            )
            for c in range(3):
                x = cells[c]
                planar = (
                    jnp.where(lanes >= 16, pltpu.roll(x, 16, 1), 0.0)
                    + jnp.where(lanes < 112, pltpu.roll(x, 112, 1), 0.0)
                    + jnp.where(column > 0, pltpu.roll(x, 1, 1), 0.0)
                    + jnp.where(column < 15, pltpu.roll(x, 127, 1), 0.0)
                )
                vertical = jnp.where(depth > 0, pltpu.roll(x, 1, 0), 0.0) + jnp.where(
                    depth < CELLS - 1, pltpu.roll(x, CELLS - 1, 0), 0.0
                )
                new = (
                    x * (common - step_length * (1.0 - couple_weight) * x * x)
                    + weight * planar
                    + grad_weight * vertical
                )
                if c == 2:
                    new = new + step_length * field_values[step]
                later[pl.ds(rows_of(c, s), CELLS), :] = new
            return carry

        lax.fori_loop(0, 8, body, 0, unroll=2)
        side_by_side = jnp.concatenate([now[pl.ds(1024 + CELLS * s, CELLS), :] for s in range(8)], axis=1)
        field = product(cv[pl.ds(ROWS, CELLS), pl.ds(0, CELLS)], side_by_side)
        for s in range(8):
            dep[pl.ds(CELLS * s, CELLS), :] = field[:, 128 * s : 128 * (s + 1)]

    def add_field(step):
        heard = jnp.concatenate([lrecv[step, pl.ds(s, ROWS, stride=8), :] for s in range(8)], axis=1)
        field = product(cv[pl.ds(ROWS + CELLS, CELLS), pl.ds(0, ROWS)], heard)
        for s in range(8):
            rows = pl.ds(CELLS * s, CELLS)
            total = dep[rows, :] + field[:, 128 * s : 128 * (s + 1)]
            if step == 1:
                dep_out[rows, :] = total
            else:
                dep[rows, :] = total

    def finish(step, c, now, later, out_ref):
        def body(s, carry):
            level = refine[s]
            factor = jnp.where(level >= 1, 4.0, 1.0) * jnp.where(level >= 2, 4.0, 1.0)
            weight = grad_weight * factor
            south_w = jnp.where(lane < 16, weight, 0.0)
            north_w = jnp.where(lane >= 112, weight, 0.0)
            west_w = jnp.where(residue == 0, weight, 0.0)
            east_w = jnp.where(residue == 15, weight, 0.0)
            x = tiles(later, c, s)
            south = faces[step][c][tab_s[16, s]]
            north = faces[step][c][tab_s[17, s]]
            west = faces[step][c][tab_s[18, s]]
            east = faces[step][c][tab_s[19, s]]
            turned = [
                pltpu.roll(jnp.where(block16 == k, south, north), (128 - 16 * k) % 128, 1)
                for k in range(8)
            ]
            mixed = jnp.where(lax.rem(lane, 2) == 1, west, east)
            sides = [pltpu.roll(mixed, (-15 - 30 * k) % 128, 1) for k in range(-1, 8)]
            for g in range(8):
                x[g] = (
                    x[g]
                    + south_w * turned[g]
                    + north_w * turned[(g + 2) % 8]
                    + west_w * sides[g + 1]
                    + east_w * sides[g]
                )
            below = jnp.where(
                my == 0,
                now[pl.ds(rows_of(c, s), 1), :],
                lrecv[step, pl.ds((NEAR + c) * 8 + s, 1), :],
            )
            above = jnp.where(
                my == COUNT - 1,
                now[pl.ds(rows_of(c, s) + CELLS - 1, 1), :],
                lrecv[step, pl.ds((SLOT + NEAR + c) * 8 + s, 1), :],
            )
            x[0] = x[0] + jnp.where(row == 0, grad_weight * below, 0.0)
            x[7] = x[7] + jnp.where(row == 7, grad_weight * above, 0.0)
            if c == 2:
                whole = dep if step == 0 else dep_out
                field = tiles(whole, 0, s)
                x = [x[g] + step_length * field[g] for g in range(8)]
            for g in range(8):
                out_ref[pl.ds(rows_of(c, s) + 8 * g, 8), :] = x[g]
            if step == 0:
                prepare(1, s, c, x)
            return carry

        lax.fori_loop(0, 8, body, 0, unroll=8)

    def wait_bytes(ref, sem):
        pltpu.make_async_copy(ref, ref, sem).wait()

    def wait_near(step):
        wait_bytes(lrecv.at[step, pl.ds(0, 2 * SLOT * 8), :], lr.at[step, 0])

    def wait_far(step):
        wait_bytes(lrecv.at[step, pl.ds(2 * SLOT * 8, (SENT - 2 * SLOT) * 8), :], lr.at[step, 1])

    def wait_strips(step, c):
        wait_bytes(faces[step][c].at[pl.ds(OWN, 30)], pr.at[step, c])

    fetch_p.wait()
    fetch_c.wait()
    functionals(0, cur)

    def first(s, carry):
        for c in range(3):
            prepare(0, s, c, tiles(cur, c, s))
        return carry

    lax.fori_loop(0, 8, first, 0)
    to_scalar.wait()
    pl.semaphore_wait(barrier, 2 * (COUNT - 1))
    send_layer(0)
    for c in range(3):
        send_strips(0, c)
    fetch_q.wait()
    fetch_l.wait()
    local_part(0, cur, nxt)
    wait_near(0)
    for c in range(3):
        wait_strips(0, c)
        if c == 2:
            wait_far(0)
            add_field(0)
        finish(0, c, cur, nxt, nxt)
        if c == 2:
            functionals(1, nxt)
            send_layer(1)
        send_strips(1, c)
    local_part(1, nxt, cur)
    wait_near(1)
    for c in range(3):
        wait_strips(1, c)
        if c == 2:
            wait_far(1)
            add_field(1)
        finish(1, c, nxt, cur, out)
    for step in range(2):
        wait_bytes(lsend.at[step, pl.ds(0, SENT * 8), :], ls.at[step])
    wait_bytes(ssend, ps.at[0])


def deliver(final, field, final_out, field_out, done):
    copies = [
        pltpu.make_async_copy(final, final_out, done.at[0]),
        pltpu.make_async_copy(field, field_out, done.at[1]),
    ]
    for copy in copies:
        copy.start()
    for copy in copies:
        copy.wait()


def on_device(polarization, quadratic, neighbours, refinement):
    vmem = pl.BlockSpec(memory_space=pltpu.VMEM)
    hbm = pl.BlockSpec(memory_space=pltpu.HBM)
    dma = pltpu.SemaphoreType.DMA
    f32 = jnp.float32
    final, field = pl.pallas_call(
        kernel,
        out_shape=(
            pltpu.VMEM((1536, 128), f32),
            pltpu.VMEM((512, 128), f32),
        ),
        in_specs=[hbm] * 5,
        out_specs=(vmem, vmem),
        scratch_shapes=[
            pltpu.SMEM((4, 8), jnp.int32),
            pltpu.VMEM((4, 8), jnp.int32),
            pltpu.SMEM((8,), jnp.int32),
            pltpu.VMEM((1536, 128), f32),
            pltpu.VMEM((1536, 128), f32),
            pltpu.VMEM((512, 128), f32),
            pltpu.VMEM((3 * CELLS, 128), f32),
            pltpu.VMEM((512, 128), f32),
            pltpu.VMEM((3, OWN, 8, 128), f32),
            *[pltpu.VMEM((OWN + 30, 8, 128), f32)] * 6,
            pltpu.VMEM((2, 3, 30, 8, 128), f32),
            pltpu.VMEM((2, ROWS * 8, 128), f32),
            pltpu.VMEM((2, ROWS * 8, 128), f32),
            pltpu.VMEM((24, 128), jnp.int32),
            pltpu.SMEM((24, 128), jnp.int32),
            dma((1,)),
            dma((2, 3)),
            dma((2,)),
            dma((2, 2)),
            dma((7,)),
        ],
        compiler_params=pltpu.CompilerParams(
            collective_id=0, has_side_effects=True, vmem_limit_bytes=32 << 20
        ),
    )(
        *(
            pltpu.with_memory_space_constraint(x, pltpu.HBM)
            for x in (
                polarization.reshape(1536, 128),
                quadratic.reshape(512, 128),
                neighbours,
                refinement,
                jnp.asarray(layer_constants()),
            )
        )
    )
    final, field = pl.pallas_call(
        deliver,
        out_shape=(
            jax.ShapeDtypeStruct((1536, 128), f32),
            jax.ShapeDtypeStruct((512, 128), f32),
        ),
        in_specs=[vmem, vmem],
        out_specs=(hbm, hbm),
        scratch_shapes=[dma((2,))],
    )(*(pltpu.with_memory_space_constraint(x, pltpu.VMEM) for x in (final, field)))
    return final.reshape(polarization.shape), field.reshape(quadratic.shape)


def solution(mesh):
    in_specs = (
        P(None, "patch", "layer", None),
        P("patch", "layer", None),
        P(None, "patch"),
        P("patch"),
    )
    out_specs = (P(None, "patch", "layer", None), P("patch", "layer", None))
    return jax.shard_map(
        on_device, mesh=mesh, in_specs=in_specs, out_specs=out_specs, check_vma=False
    )
```

```python
import functools
import math

import jax
import jax.numpy as jnp
import numpy as np
from jax import lax
from jax.experimental import pallas as pl
from jax.experimental.pallas import tpu as pltpu
from jax.sharding import PartitionSpec as P

step_length = 0.1
grad_weight = 0.01
couple_weight = 0.5
screening = 0.0001
damping = 2.0 / 3.0
field_values = (0.8 * math.sin(0.6 * math.pi), 0.8 * math.sin(0.8 * math.pi))

MESH = pl.DeviceIdType.MESH
HIGHEST = lax.Precision.HIGHEST

CELLS = 64
COUNT = 16
NEAR = 13
SLOT = 16
SENT = 60
ROWS = 64
OWN = 24

PARTNERS = sorted(
    [(dx, dy) for dx in range(4) for dy in range(4) if dx or dy],
    key=lambda d: -(min(d[0], 4 - d[0]) + min(d[1], 4 - d[1])),
)
MESSAGES = {1: (0, NEAR), COUNT - 1: (SLOT, NEAR), 2: (2 * SLOT, 3), COUNT - 2: (2 * SLOT + 3, 3)}
MESSAGES.update({o: (2 * SLOT + 2 * o, 2) for o in range(3, COUNT - 2)})
FARTHER = sorted(range(2, COUNT - 1), key=lambda o: -min(o, COUNT - o))


def column_cycle(source, level):
    diagonal = 2.0 * 0.25**level + screening
    if source.shape[0] == 1:
        return source / diagonal

    def apply(v):
        padded = np.pad(v, ((1, 1), (0, 0)))
        return (2.0 * v - padded[:-2] - padded[2:]) * 0.25**level + screening * v

    correction = damping * source / diagonal
    residual = source - apply(correction)
    coarse = (residual[0::2] + residual[1::2]) * 0.5
    correction = correction + np.repeat(column_cycle(coarse, level + 1), 2, axis=0)
    return correction + damping * (source - apply(correction)) / diagonal


def field_operator(cells):
    padded = np.pad(np.eye(cells), ((1, 1), (0, 0)), mode="edge")
    charge = -(padded[2:] - padded[:-2]) * 0.5
    rimmed = np.pad(column_cycle(charge, 0), ((1, 1), (0, 0)))
    return -(rimmed[2:] - rimmed[:-2]) * 0.5


def row_basis(block, rank):
    rest = block.copy()
    rows = np.zeros((rank, block.shape[1]))
    for k in range(rank):
        norms = np.sum(rest * rest, axis=1)
        best = int(np.argmax(norms))
        if norms[best] < 1e-24:
            break
        row = rest[best]
        for _ in range(2):
            for earlier in rows[:k]:
                row = row - np.sum(row * earlier) * earlier
        row = row / np.sqrt(np.sum(row * row))
        rows[k] = row
        rest = rest - np.sum(rest * row, axis=1, keepdims=True) * row
    return rows


def project(block, rows):
    return np.stack([np.sum(block * row, axis=1) for row in rows], axis=1)


@functools.cache
def layer_constants():
    whole = field_operator(CELLS * COUNT)

    def block(d, e):
        return whole[d * CELLS : (d + 1) * CELLS, e * CELLS : (e + 1) * CELLS]

    table = np.zeros((COUNT, 3 * CELLS, 128))
    for e in range(COUNT):
        table[e, ROWS : ROWS + CELLS, :CELLS] = block(e, e)
        for o, (first, rank) in MESSAGES.items():
            d = (e + o) % COUNT
            basis = row_basis(block(d, e), rank)
            table[e, first : first + rank, :CELLS] = basis
            table[d, ROWS + CELLS :, first : first + rank] = project(block(d, e), basis)
    return table.astype(np.float32)


def product(left, right):
    def split(x):
        high = x.astype(jnp.bfloat16)
        return high, (x - high.astype(jnp.float32)).astype(jnp.bfloat16)

    def dot(a, b):
        return jnp.dot(a, b, preferred_element_type=jnp.float32)

    (lh, ll), (rh, rl) = split(left), split(right)
    return dot(lh, rh) + (dot(lh, rl) + dot(ll, rh))


def kernel(
    pol, quad, nbr, levels, consts,
    out, dep_out,
    nbr_s, nbr_v, refine, cur, nxt, qv, cv, dep, mine,
    faces00, faces01, faces02, faces10, faces11, faces12,
    ssend, lsend, lrecv, tab_v, tab_s, ps, pr, ls, lr, local,
):
    faces = ((faces00, faces01, faces02), (faces10, faces11, faces12))
    me = lax.axis_index("patch")
    my = lax.axis_index("layer")
    mx, my_y = me // 4, lax.rem(me, 4)

    def patch_peer(dx, dy):
        return (lax.rem(mx + dx, 4) * 4 + lax.rem(my_y + dy, 4), my)

    def layer_peer(o):
        return (me, lax.rem(my + o, COUNT))

    barrier = pltpu.get_barrier_semaphore()
    for dx, dy in PARTNERS:
        pl.semaphore_signal(barrier, inc=1, device_id=patch_peer(dx, dy), device_id_type=MESH)
    for o in range(1, COUNT):
        pl.semaphore_signal(barrier, inc=1, device_id=layer_peer(o), device_id_type=MESH)

    fetch_p = pltpu.make_async_copy(pol, cur, local.at[0])
    fetch_c = pltpu.make_async_copy(consts.at[my], cv, local.at[1])
    fetch_q = pltpu.make_async_copy(quad, qv, local.at[2])
    fetch_n = pltpu.make_async_copy(nbr, nbr_s, local.at[4])
    fetch_v = pltpu.make_async_copy(nbr, nbr_v, local.at[5])
    fetch_l = pltpu.make_async_copy(levels, refine, local.at[6])
    fetch_n.start()
    fetch_v.start()
    fetch_p.start()
    fetch_c.start()
    fetch_l.start()
    fetch_q.start()

    lane = lax.broadcasted_iota(jnp.int32, (8, 128), 1)
    row = lax.broadcasted_iota(jnp.int32, (8, 128), 0)
    block16 = lane // 16
    residue = lax.rem(lane, 16)

    def relative(device):
        return lax.rem(device // 4 - mx + 4, 4) * 4 + lax.rem(lax.rem(device, 4) - my_y + 4, 4)

    fetch_n.wait()
    fetch_v.wait()
    face = lax.broadcasted_iota(jnp.int32, (4, 8), 0)
    there = nbr_v[...]
    device = there // 8
    mirrored = face + 1 - 2 * lax.rem(face, 2)
    key = mirrored * 8 + lax.rem(there, 8)
    rank = jnp.zeros((4, 8), jnp.int32)
    least = jnp.zeros((8, 128), jnp.int32)
    most = jnp.zeros((8, 128), jnp.int32)
    for f in range(4):
        for s in range(8):
            n = nbr_s[f, s]
            other_key = (f ^ 1) * 8 + lax.rem(n, 8)
            before = (device == n // 8) & (key > other_key)
            rank = rank + jnp.where(before, 1, 0)
            most = jnp.where(lane == relative(n // 8), f * 8 + s, most)
            n = nbr_s[3 - f, 7 - s]
            least = jnp.where(lane == relative(n // 8), (3 - f) * 8 + 7 - s, least)
    place = jnp.where(
        device == me,
        jnp.minimum(mirrored, 2) * 8 + lax.rem(there, 8),
        OWN + (relative(device) - 1) * 2 + jnp.minimum(rank, 1),
    )
    tab_v[pl.ds(0, 8), :] = jnp.where(least >= 24, least - 8, least)
    tab_v[pl.ds(8, 8), :] = jnp.where(most >= 24, most - 8, most)
    tab_v[pl.ds(16, 4), pl.ds(0, 8)] = place
    to_scalar = pltpu.make_async_copy(tab_v, tab_s, local.at[3])
    to_scalar.start()

    for step in range(2):
        lrecv[step, pl.ds((ROWS - 4) * 8, 32), :] = jnp.zeros((32, 128), jnp.float32)

    def rows_of(c, s):
        return pl.multiple_of(c * 512 + s * CELLS, CELLS)

    def prepare(step, s, c, cells):
        high, low, sides = cells[7], cells[7], cells[0]
        for g in range(7):
            turned = pltpu.roll(cells[g], 16 * (g + 1), 1)
            high = jnp.where(block16 == g, turned, high)
            low = jnp.where(block16 == g + 1, turned, low)
        for g in range(1, 8):
            turned = pltpu.roll(cells[g], (30 * g) % 128, 1)
            sides = jnp.where(
                (residue == 16 - 2 * g) | (residue == 15 - 2 * g), turned, sides
            )
        mine[c, s] = low
        mine[c, 8 + s] = high
        mine[c, 16 + s] = sides
        faces[step][c][s] = low
        faces[step][c][8 + s] = high
        faces[step][c][16 + s] = sides
        lsend[step, pl.ds((NEAR + c) * 8 + s, 1), :] = cells[7][7:8]
        lsend[step, pl.ds((SLOT + NEAR + c) * 8 + s, 1), :] = cells[0][0:1]

    def functionals(step, now):
        side_by_side = jnp.concatenate([now[pl.ds(1024 + CELLS * s, CELLS), :] for s in range(8)], axis=1)
        got = product(cv[pl.ds(0, ROWS), pl.ds(0, CELLS)], side_by_side)
        for s in range(8):
            part = got[:, 128 * s : 128 * (s + 1)]
            lsend[step, pl.ds(s, NEAR, stride=8), :] = part[:NEAR]
            lsend[step, pl.ds(SLOT * 8 + s, NEAR, stride=8), :] = part[SLOT : SLOT + NEAR]
            lsend[step, pl.ds(2 * SLOT * 8 + s, 32, stride=8), :] = part[2 * SLOT :]

    def send_layer(step):
        pieces = []
        for part in range(4):
            for o in (1, COUNT - 1):
                pieces.append((o, MESSAGES[o][0] + part * SLOT // 4, SLOT // 4))
        pieces += [(o, *MESSAGES[o]) for o in FARTHER]
        for o, first, count in pieces:
            rows = pl.ds(first * 8, count * 8)
            pltpu.make_async_remote_copy(
                src_ref=lsend.at[step, rows, :],
                dst_ref=lrecv.at[step, rows, :],
                send_sem=ls.at[step],
                recv_sem=lr.at[step, 0 if o in (1, COUNT - 1) else 1],
                device_id=layer_peer(o),
                device_id_type=MESH,
            ).start()

    def send_strips(step, c):
        for dx, dy in PARTNERS:
            to = dx * 4 + dy
            back = (4 - dx) % 4 * 4 + (4 - dy) % 4
            ssend[step, c, 2 * to - 2] = mine[c, tab_s[0, to]]
            ssend[step, c, 2 * to - 1] = mine[c, tab_s[8, to]]
            pltpu.make_async_remote_copy(
                src_ref=ssend.at[step, c, pl.ds(2 * to - 2, 2)],
                dst_ref=faces[step][c].at[pl.ds(OWN + 2 * back - 2, 2)],
                send_sem=ps.at[0],
                recv_sem=pr.at[step, c],
                device_id=patch_peer(dx, dy),
                device_id_type=MESH,
            ).start()

    def tiles(ref, c, s):
        return [ref[pl.ds(rows_of(c, s) + 8 * g, 8), :] for g in range(8)]

    def local_part(step, now, later):
        def body(s, carry):
            level = refine[s]
            factor = jnp.where(level >= 1, 4.0, 1.0) * jnp.where(level >= 2, 4.0, 1.0)
            weight = grad_weight * factor
            cells = [now[pl.ds(rows_of(c, s), CELLS), :] for c in range(3)]
            lanes = lax.broadcasted_iota(jnp.int32, (CELLS, 128), 1)
            depth = lax.broadcasted_iota(jnp.int32, (CELLS, 128), 0)
            column = lax.rem(lanes, 16)
            square = cells[0] * cells[0] + cells[1] * cells[1] + cells[2] * cells[2]
            common = (
                1.0
                - 2.0 * grad_weight
                - 4.0 * weight
                - step_length * qv[pl.ds(pl.multiple_of(s * CELLS, CELLS), CELLS), :]
                - step_length * couple_weight * square
            )
            for c in range(3):
                x = cells[c]
                planar = (
                    jnp.where(lanes >= 16, pltpu.roll(x, 16, 1), 0.0)
                    + jnp.where(lanes < 112, pltpu.roll(x, 112, 1), 0.0)
                    + jnp.where(column > 0, pltpu.roll(x, 1, 1), 0.0)
                    + jnp.where(column < 15, pltpu.roll(x, 127, 1), 0.0)
                )
                vertical = jnp.where(depth > 0, pltpu.roll(x, 1, 0), 0.0) + jnp.where(
                    depth < CELLS - 1, pltpu.roll(x, CELLS - 1, 0), 0.0
                )
                new = (
                    x * (common - step_length * (1.0 - couple_weight) * x * x)
                    + weight * planar
                    + grad_weight * vertical
                )
                if c == 2:
                    new = new + step_length * field_values[step]
                later[pl.ds(rows_of(c, s), CELLS), :] = new
            return carry

        lax.fori_loop(0, 8, body, 0, unroll=2)
        side_by_side = jnp.concatenate([now[pl.ds(1024 + CELLS * s, CELLS), :] for s in range(8)], axis=1)
        field = product(cv[pl.ds(ROWS, CELLS), pl.ds(0, CELLS)], side_by_side)
        for s in range(8):
            dep[pl.ds(CELLS * s, CELLS), :] = field[:, 128 * s : 128 * (s + 1)]

    def add_field(step):
        heard = jnp.concatenate([lrecv[step, pl.ds(s, ROWS, stride=8), :] for s in range(8)], axis=1)
        field = product(cv[pl.ds(ROWS + CELLS, CELLS), pl.ds(0, ROWS)], heard)
        for s in range(8):
            rows = pl.ds(CELLS * s, CELLS)
            total = dep[rows, :] + field[:, 128 * s : 128 * (s + 1)]
            if step == 1:
                dep_out[rows, :] = total
            else:
                dep[rows, :] = total

    def finish(step, c, now, later, out_ref):
        def body(s, carry):
            level = refine[s]
            factor = jnp.where(level >= 1, 4.0, 1.0) * jnp.where(level >= 2, 4.0, 1.0)
            weight = grad_weight * factor
            south_w = jnp.where(lane < 16, weight, 0.0)
            north_w = jnp.where(lane >= 112, weight, 0.0)
            west_w = jnp.where(residue == 0, weight, 0.0)
            east_w = jnp.where(residue == 15, weight, 0.0)
            x = tiles(later, c, s)
            south = faces[step][c][tab_s[16, s]]
            north = faces[step][c][tab_s[17, s]]
            west = faces[step][c][tab_s[18, s]]
            east = faces[step][c][tab_s[19, s]]
            turned = [
                pltpu.roll(jnp.where(block16 == k, south, north), (128 - 16 * k) % 128, 1)
                for k in range(8)
            ]
            mixed = jnp.where(lax.rem(lane, 2) == 1, west, east)
            sides = [pltpu.roll(mixed, (-15 - 30 * k) % 128, 1) for k in range(-1, 8)]
            for g in range(8):
                x[g] = (
                    x[g]
                    + south_w * turned[g]
                    + north_w * turned[(g + 2) % 8]
                    + west_w * sides[g + 1]
                    + east_w * sides[g]
                )
            below = jnp.where(
                my == 0,
                now[pl.ds(rows_of(c, s), 1), :],
                lrecv[step, pl.ds((NEAR + c) * 8 + s, 1), :],
            )
            above = jnp.where(
                my == COUNT - 1,
                now[pl.ds(rows_of(c, s) + CELLS - 1, 1), :],
                lrecv[step, pl.ds((SLOT + NEAR + c) * 8 + s, 1), :],
            )
            x[0] = x[0] + jnp.where(row == 0, grad_weight * below, 0.0)
            x[7] = x[7] + jnp.where(row == 7, grad_weight * above, 0.0)
            if c == 2:
                whole = dep if step == 0 else dep_out
                field = tiles(whole, 0, s)
                x = [x[g] + step_length * field[g] for g in range(8)]
            for g in range(8):
                out_ref[pl.ds(rows_of(c, s) + 8 * g, 8), :] = x[g]
            if step == 0:
                prepare(1, s, c, x)
            return carry

        lax.fori_loop(0, 8, body, 0, unroll=8)

    def wait_bytes(ref, sem):
        pltpu.make_async_copy(ref, ref, sem).wait()

    def wait_near(step):
        wait_bytes(lrecv.at[step, pl.ds(0, 2 * SLOT * 8), :], lr.at[step, 0])

    def wait_far(step):
        wait_bytes(lrecv.at[step, pl.ds(2 * SLOT * 8, (SENT - 2 * SLOT) * 8), :], lr.at[step, 1])

    def wait_strips(step, c):
        wait_bytes(faces[step][c].at[pl.ds(OWN, 30)], pr.at[step, c])

    fetch_p.wait()
    fetch_c.wait()
    functionals(0, cur)

    def first(s, carry):
        for c in range(3):
            prepare(0, s, c, tiles(cur, c, s))
        return carry

    lax.fori_loop(0, 8, first, 0)
    to_scalar.wait()
    pl.semaphore_wait(barrier, 2 * (COUNT - 1))
    send_layer(0)
    for c in range(3):
        send_strips(0, c)
    fetch_q.wait()
    fetch_l.wait()
    local_part(0, cur, nxt)
    wait_near(0)
    for c in range(3):
        wait_strips(0, c)
        if c == 2:
            wait_far(0)
            add_field(0)
        finish(0, c, cur, nxt, nxt)
        if c == 2:
            functionals(1, nxt)
            send_layer(1)
        send_strips(1, c)
    local_part(1, nxt, cur)
    wait_near(1)
    for c in range(3):
        wait_strips(1, c)
        if c == 2:
            wait_far(1)
            add_field(1)
        finish(1, c, nxt, cur, out)
    for step in range(2):
        wait_bytes(lsend.at[step, pl.ds(0, SENT * 8), :], ls.at[step])
    wait_bytes(ssend, ps.at[0])


def deliver(final, field, final_out, field_out, done):
    copies = [
        pltpu.make_async_copy(final, final_out, done.at[0]),
        pltpu.make_async_copy(field, field_out, done.at[1]),
    ]
    for copy in copies:
        copy.start()
    for copy in copies:
        copy.wait()


def on_device(polarization, quadratic, neighbours, refinement):
    vmem = pl.BlockSpec(memory_space=pltpu.VMEM)
    hbm = pl.BlockSpec(memory_space=pltpu.HBM)
    dma = pltpu.SemaphoreType.DMA
    f32 = jnp.float32
    final, field = pl.pallas_call(
        kernel,
        out_shape=(
            pltpu.VMEM((1536, 128), f32),
            pltpu.VMEM((512, 128), f32),
        ),
        in_specs=[hbm] * 5,
        out_specs=(vmem, vmem),
        scratch_shapes=[
            pltpu.SMEM((4, 8), jnp.int32),
            pltpu.VMEM((4, 8), jnp.int32),
            pltpu.SMEM((8,), jnp.int32),
            pltpu.VMEM((1536, 128), f32),
            pltpu.VMEM((1536, 128), f32),
            pltpu.VMEM((512, 128), f32),
            pltpu.VMEM((3 * CELLS, 128), f32),
            pltpu.VMEM((512, 128), f32),
            pltpu.VMEM((3, OWN, 8, 128), f32),
            *[pltpu.VMEM((OWN + 30, 8, 128), f32)] * 6,
            pltpu.VMEM((2, 3, 30, 8, 128), f32),
            pltpu.VMEM((2, ROWS * 8, 128), f32),
            pltpu.VMEM((2, ROWS * 8, 128), f32),
            pltpu.VMEM((24, 128), jnp.int32),
            pltpu.SMEM((24, 128), jnp.int32),
            dma((1,)),
            dma((2, 3)),
            dma((2,)),
            dma((2, 2)),
            dma((7,)),
        ],
        compiler_params=pltpu.CompilerParams(
            collective_id=0, has_side_effects=True, vmem_limit_bytes=32 << 20
        ),
    )(
        *(
            pltpu.with_memory_space_constraint(x, pltpu.HBM)
            for x in (
                polarization.reshape(1536, 128),
                quadratic.reshape(512, 128),
                neighbours,
                refinement,
                jnp.asarray(layer_constants()),
            )
        )
    )
    final, field = pl.pallas_call(
        deliver,
        out_shape=(
            jax.ShapeDtypeStruct((1536, 128), f32),
            jax.ShapeDtypeStruct((512, 128), f32),
        ),
        in_specs=[vmem, vmem],
        out_specs=(hbm, hbm),
        scratch_shapes=[dma((2,))],
    )(*(pltpu.with_memory_space_constraint(x, pltpu.VMEM) for x in (final, field)))
    return final.reshape(polarization.shape), field.reshape(quadratic.shape)


def solution(mesh):
    in_specs = (
        P(None, "patch", "layer", None),
        P("patch", "layer", None),
        P(None, "patch"),
        P("patch"),
    )
    out_specs = (P(None, "patch", "layer", None), P("patch", "layer", None))
    return jax.shard_map(
        on_device, mesh=mesh, in_specs=in_specs, out_specs=out_specs, check_vma=False
    )
```
